32 devices in a mesh: depth: 4 (over z), lateral: 8 (over y, x, core).
Axes of the slice: x: 2, y: 2, z: 4, core: 2. Of those that a mesh axis runs over, the one named last changes fastest.
Arguments:
- samples: bfloat16 [4, 8, 64, 8192], P('depth', 'lateral'), may hold values from -6 to 6
- w_first: bfloat16 [4, 8, 64, 256], P('depth', 'lateral'), may hold values from -0.75 to 0.75
- w_second: bfloat16 [4, 8, 256, 256], P('depth', 'lateral'), may hold values from -0.5 to 0.5
- w_third: bfloat16 [4, 8, 256, 512], P('depth', 'lateral'), may hold values from -0.5 to 0.5
- w_density: bfloat16 [4, 8, 256], P('depth', 'lateral'), may hold values from -0.5 to 0.5
- decoder: float32 [8, 3, 512], P('lateral'), may hold values from -1 to 1
- depth_order: int32 [8, 4], P('lateral'), may hold values from 0 to 3, each once within a row
- ray_slot: int32 [8, 1024], P('lateral'), may hold values from 0 to 255, as said below
- target: float32 [8, 3, 256], P('lateral', None, 'depth'), may hold values from -24 to 24
Outputs:
- grad_first: float32 [4, 8, 64, 256], P('depth', 'lateral')
- grad_second: float32 [4, 8, 256, 256], P('depth', 'lateral')
- grad_third: float32 [4, 8, 256, 512], P('depth', 'lateral')
- grad_density: float32 [4, 8, 256], P('depth', 'lateral')
- grad_decoder: float32 [8, 3, 512], P('lateral')
- mean_error: float32 [], replicated
The draws below stay inside these ranges and needn't reach their ends.
Inputs may be any that keep to these rules, and one draw needn't show every extreme that they name: `ray_slot`: in each row, every aligned block of 256 entries holds each of 0 to 255 once. `depth_order`: each row names every tile once.
All inputs are finite; a program needn't handle non-finite values.
Results may differ from the reference program's by a relative error of at most 0.017.
The reference program's roundings to bfloat16 on the way (of `features`, `scaled`, `ray_feature`, `ray_grad`, `logit_grad`, `feature_grad`, `back_two` and `back_one`) count: a program that leaves them out, or rounds other values in their place, can miss the bound.
Values may be sent and summed in bfloat16 or wider, within the bound.
No kernel may reach another device: no remote copies, remote signals or barrier semaphores. Data moves between devices by JAX's collectives and lax.ppermute only.
A program may use at most 128 MiB of HBM per device.

```python
import jax
import jax.numpy as jnp
from jax import lax

ENC = 64
HID = 256
FEAT = 512
SAMPLES = 8
SPP = 4
RAYS = 1024
TILES = 4
COLS = 8
SHARE = 256
SLOTS = 32
PIXELS = 256
PIX_SHARE = 64


def draw_ray_slot(key, part):
    blocks = jax.random.split(key, COLS * TILES)
    orders = jax.vmap(lambda single: jax.random.permutation(single, SHARE))(blocks)
    return orders.reshape(COLS, RAYS).astype(jnp.int32)


def draw_target(key, part):
    inner = jax.random.fold_in(key, 7)
    pixel_pos = jnp.arange(PIXELS, dtype=jnp.float32) / max(PIXELS - 1, 1)
    column_pos = jnp.arange(COLS, dtype=jnp.float32) / max(COLS - 1, 1)
    rising = (0.4 + 1.6 * column_pos)[:, None, None] * (0.4 + 1.6 * pixel_pos)[None, None, :]
    noise = jnp.clip(jax.random.normal(inner, (COLS, 3, PIXELS), jnp.float32), -6.0, 6.0)
    return (noise * rising).astype(jnp.float32)


def block_levels(rng, shape, shards, smallest, largest):
    def one(position, blocks):
        heights = jax.random.uniform(jax.random.fold_in(jax.random.fold_in(rng, 6), position), (blocks,), jnp.float32, smallest / len(shards), largest / len(shards))
        return jnp.repeat(jnp.exp(heights), shape[position] // blocks).reshape((-1,) + (1,) * (len(shape) - position - 1))

    gain = one(*shards[0])
    for cut in shards[1:]:
        gain = gain * one(*cut)
    return gain


def normal_values(rng, dims, spread, reach, cuts=(), kind=jnp.bfloat16):
    drawn = jax.random.normal(rng, dims, jnp.float32) * spread
    if len(cuts) > 0:
        drawn = block_levels(rng, dims, cuts, -0.22, 0.18) * drawn
    return jnp.clip(drawn, min=-reach, max=reach).astype(kind)


def setup_inputs(seed: int = 0) -> dict:
    arg_keys = jax.random.split(jax.random.key(seed), 10)
    samples = normal_values(arg_keys[0], (TILES, COLS, ENC, SAMPLES * RAYS), 1.0, 6.0, ((0, 4), (1, 8)))
    w_first = normal_values(arg_keys[1], (TILES, COLS, ENC, HID), ENC ** -0.5, 0.75, ((0, 4), (1, 8)))
    w_second = normal_values(arg_keys[2], (TILES, COLS, HID, HID), (HID // 2) ** -0.5, 0.5, ((0, 4), (1, 8)))
    w_third = normal_values(arg_keys[3], (TILES, COLS, HID, FEAT), (HID // 2) ** -0.5, 0.5, ((0, 4), (1, 8)))
    w_density = normal_values(arg_keys[4], (TILES, COLS, HID), (HID // 2) ** -0.5, 0.5, ((0, 4), (1, 8)))
    decoder = normal_values(arg_keys[5], (COLS, 3, FEAT), (FEAT // 16) ** -0.5, 1.0, ((0, 8),), jnp.float32)
    depth_order = jax.vmap(lambda own: jax.random.permutation(own, TILES))(jax.random.split(arg_keys[6], COLS)).reshape((COLS, TILES)).astype(jnp.int32)
    ray_slot = draw_ray_slot(jax.random.fold_in(arg_keys[9], 71), 0)
    target = draw_target(jax.random.fold_in(arg_keys[9], 71), 0)
    return {"samples": samples, "w_first": w_first, "w_second": w_second, "w_third": w_third, "w_density": w_density, "decoder": decoder, "depth_order": depth_order, "ray_slot": ray_slot, "target": target}


step_length = 0.04
norm_floor = 1e-05
exact_mode = lax.Precision.HIGHEST

def network(inputs, w_first, w_second, w_third, w_density):
    contract_lead = (((0,), (0,)), ((), ()))
    hidden_one = jnp.maximum(lax.dot_general(w_first, inputs, contract_lead, preferred_element_type=jnp.float32), 0.0).astype(jnp.bfloat16)
    hidden_two = jnp.maximum(lax.dot_general(w_second, hidden_one, contract_lead, preferred_element_type=jnp.float32), 0.0).astype(jnp.bfloat16)
    features = lax.dot_general(w_third, hidden_two, contract_lead, preferred_element_type=jnp.float32).astype(jnp.bfloat16)
    logits = jnp.dot(w_density, hidden_two, preferred_element_type=jnp.float32)
    return (hidden_one, hidden_two, features, logits)

def segment(density):
    before_here = step_length * (jnp.cumsum(density, axis=0) - density)
    weights = jnp.exp(-before_here) * (1.0 - jnp.exp(-step_length * density))
    return (weights, step_length * lax.optimization_barrier(jnp.sum(density, axis=0)))

def blend_samples(features, weights):
    sample_count = weights.shape[0]
    blocks = features.reshape(features.shape[0], sample_count, weights.shape[1])
    total = jnp.zeros((features.shape[0], weights.shape[1]), jnp.float32)
    for sample in range(sample_count):
        total = total + blocks[:, sample].astype(jnp.float32) * weights[sample][None]
    return total

def tile_forward(inputs, w_first, w_second, w_third, w_density, sample_count):
    hidden_one, hidden_two, features, logits = network(inputs, w_first, w_second, w_third, w_density)
    density = jax.nn.softplus(logits).reshape(sample_count, -1)
    weights, depth_sum = segment(density)
    return (hidden_one, hidden_two, features, logits, weights, depth_sum)

def tile_backward(inputs, w_first, w_second, w_third, w_density, hidden_one, hidden_two, features, logits, feat_grad, depth_grad, sample_count):
    density = jax.nn.softplus(logits).reshape(sample_count, -1)
    outputs, pullback = jax.vjp(segment, density)
    weights = outputs[0]
    blocks = features.reshape(features.shape[0], sample_count, -1)
    weight_grad = jnp.stack([lax.optimization_barrier(jnp.sum(blocks[:, sample].astype(jnp.float32) * feat_grad, axis=0)) for sample in range(sample_count)])
    density_grad = pullback((weight_grad, depth_grad))[0]
    logit_grad = (density_grad * jax.nn.sigmoid(logits.reshape(sample_count, -1))).reshape(-1).astype(jnp.bfloat16)
    feature_grad = (weights[None] * feat_grad[:, None]).astype(jnp.bfloat16).reshape(features.shape)
    contract_rows = (((1,), (1,)), ((), ()))
    grad_third = lax.dot_general(hidden_two, feature_grad, contract_rows, preferred_element_type=jnp.float32)
    grad_density = jnp.dot(hidden_two, logit_grad, preferred_element_type=jnp.float32)
    back_two = jnp.dot(w_third, feature_grad, preferred_element_type=jnp.float32)
    back_two = back_two + w_density.astype(jnp.float32)[:, None] * logit_grad.astype(jnp.float32)[None]
    back_two = jnp.where(hidden_two > 0, back_two, 0.0).astype(jnp.bfloat16)
    grad_second = lax.dot_general(hidden_one, back_two, contract_rows, preferred_element_type=jnp.float32)
    back_one = jnp.where(hidden_one > 0, jnp.dot(w_second, back_two, preferred_element_type=jnp.float32), 0.0).astype(jnp.bfloat16)
    grad_first = lax.dot_general(inputs, back_one, contract_rows, preferred_element_type=jnp.float32)
    return (grad_first, grad_second, grad_third, grad_density)

def reference(samples, w_first, w_second, w_third, w_density, decoder, depth_order, ray_slot, target):

    def forward_column(column):

        def forward_tile(tile):
            outputs = tile_forward(samples[tile, column], w_first[tile, column], w_second[tile, column], w_third[tile, column], w_density[tile, column], SAMPLES)
            return (blend_samples(outputs[2], outputs[4]), outputs[5])
        return lax.map(forward_tile, jnp.arange(TILES, dtype=jnp.int32))
    blended, depth_sums = lax.map(forward_column, jnp.arange(COLS, dtype=jnp.int32))
    ranks = jnp.arange(TILES, dtype=jnp.int32)
    places = lax.optimization_barrier(jnp.sum(ranks[None, :, None] * (depth_order[:, :, None] == ranks[None, None, :]).astype(jnp.int32), axis=1))
    earlier = (places[:, None, :] < places[:, :, None]).astype(jnp.float32)
    before = jnp.einsum('ckj,cjr->ckr', earlier, depth_sums, precision=exact_mode)
    scale = jnp.exp(-before)
    scaled = (scale[:, :, None, :] * blended).astype(jnp.bfloat16)
    ray_feature = lax.optimization_barrier(jnp.sum(scaled.astype(jnp.float32), axis=1)).astype(jnp.bfloat16)
    ray_index = jnp.arange(RAYS, dtype=jnp.int32)
    columns = jnp.arange(COLS, dtype=jnp.int32)[:, None]
    owner = ray_slot // SLOTS
    inside = ray_slot % SLOTS
    pixel_id = owner * PIXELS + (ray_index // SHARE)[None] * PIX_SHARE + (inside * COLS + columns) // SPP
    rows = jnp.swapaxes(ray_feature.astype(jnp.float32), 1, 2).reshape(COLS * RAYS, FEAT)
    pixel_rows = jax.ops.segment_sum(rows, pixel_id.reshape(-1), num_segments=COLS * PIXELS) / SPP
    pixel_mean = jnp.swapaxes(pixel_rows.reshape(COLS, PIXELS, FEAT), 1, 2)
    inverse = lax.rsqrt(lax.optimization_barrier(jnp.mean(pixel_mean * pixel_mean, axis=1, keepdims=True)) + norm_floor)
    normed = pixel_mean * inverse
    colors = jnp.einsum('cif,cfp->cip', decoder, normed, precision=exact_mode)
    residue = colors - target
    mean_error = jnp.sum(residue * residue) / (3 * COLS * PIXELS)
    grad_decoder = jnp.einsum('cip,cfp->cif', residue, normed, precision=exact_mode)
    normed_grad = jnp.einsum('cif,cip->cfp', decoder, residue, precision=exact_mode)
    pixel_grad = inverse * (normed_grad - normed * lax.optimization_barrier(jnp.mean(normed_grad * normed, axis=1, keepdims=True))) / SPP
    pixel_grad = jnp.swapaxes(pixel_grad, 1, 2)
    ray_grad = jnp.swapaxes(pixel_grad.reshape(COLS * PIXELS, FEAT)[pixel_id], 1, 2).astype(jnp.bfloat16)
    terms = jnp.einsum('ckfr,cfr->ckr', scaled.astype(jnp.float32), ray_grad.astype(jnp.float32))
    depth_grads = -jnp.einsum('cmk,cmr->ckr', earlier, terms, precision=exact_mode)

    def backward_column(column):

        def backward_tile(tile):
            inputs = samples[tile, column]
            weights_a = w_first[tile, column]
            weights_b = w_second[tile, column]
            weights_c = w_third[tile, column]
            weights_d = w_density[tile, column]
            outputs = tile_forward(inputs, weights_a, weights_b, weights_c, weights_d, SAMPLES)
            feat_grad = scale[column, tile][None] * ray_grad[column].astype(jnp.float32)
            return tile_backward(inputs, weights_a, weights_b, weights_c, weights_d, outputs[0], outputs[1], outputs[2], outputs[3], feat_grad, depth_grads[column, tile], SAMPLES)
        return lax.map(backward_tile, jnp.arange(TILES, dtype=jnp.int32))
    grad_first, grad_second, grad_third, grad_density = lax.map(backward_column, jnp.arange(COLS, dtype=jnp.int32))
    return (jnp.swapaxes(grad_first, 0, 1), jnp.swapaxes(grad_second, 0, 1), jnp.swapaxes(grad_third, 0, 1), jnp.swapaxes(grad_density, 0, 1), grad_decoder, mean_error)
```

```python
import functools

import jax
import jax.numpy as jnp
from jax import lax
from jax.experimental import pallas as pl
from jax.experimental.pallas import tpu as pltpu
from jax.sharding import Mesh
from jax.sharding import PartitionSpec as P

SAMPLES = 8
SPP = 4
PAIR = 2

step_length = 0.04
norm_floor = 1e-05
exact_mode = lax.Precision.HIGHEST
vmem_grant = 48 * 1024 * 1024

rows_rows = (((1,), (1,)), ((), ()))
lead_lead = (((0,), (0,)), ((), ()))


def dot(left, right, **how):
    return jnp.dot(left, right, preferred_element_type=jnp.float32, **how)


def dot_rows(left, right, **how):
    return lax.dot_general(left, right, rows_rows, preferred_element_type=jnp.float32, **how)


def softplus(value):
    return jnp.maximum(value, 0.0) + jnp.log1p(jnp.exp(-jnp.abs(value)))


def tile_place(order_ref, tile, tile_count):
    place = jnp.int32(0)
    for position in range(tile_count):
        place = place + jnp.where(order_ref[0, position] == tile, position, 0)
    return place


def forward_kernel(
    share,
    slot_rays,
    samples_ref,
    slot_ref,
    first_ref,
    second_ref,
    density_ref,
    routed_ref,
    one_ref,
    two_ref,
    logit_ref,
    gathered_ref,
    sum_ref,
    route_ref,
    first_turned,
    second_turned,
    passed_ref,
):
    sample = pl.program_id(0)
    rays = samples_ref.shape[1]
    shares = rays // share

    @pl.when(sample == 0)
    def prepare():
        me = lax.axis_index("core")
        target_row = lax.broadcasted_iota(jnp.int32, (share, share), 0)
        for part in range(shares):
            slots = slot_ref[:, part * share : (part + 1) * share]
            owner = lax.div(slots, jnp.int32(slot_rays))
            inside = slots - owner * slot_rays
            lateral = lax.div(owner, jnp.int32(PAIR))
            side = jnp.bitwise_xor(owner - lateral * PAIR, me)
            place = side * (share // PAIR) + lateral * slot_rays + inside
            route_ref[part] = (target_row == place).astype(jnp.float32).astype(jnp.bfloat16)
        first_turned[...] = first_ref[...].T
        second_turned[...] = second_ref[...].T
        passed_ref[...] = jnp.zeros_like(passed_ref)
        gathered_ref[...] = jnp.zeros_like(gathered_ref)

    for part in range(shares):
        lanes = slice(part * share, (part + 1) * share)
        routed = dot_rows(samples_ref[:, lanes], route_ref[part]).astype(jnp.bfloat16)
        routed_ref[:, lanes] = routed
        one = jnp.maximum(dot(first_turned[...], routed), 0.0).astype(jnp.bfloat16)
        one_ref[:, lanes] = one
        two = jnp.maximum(dot(second_turned[...], one), 0.0).astype(jnp.bfloat16)
        two_ref[:, lanes] = two
        logits = dot(density_ref[...], two)
        logit_ref[:, lanes] = logits
        density = softplus(logits)
        passed = passed_ref[:, lanes]
        weights = jnp.exp(-step_length * passed) * (1.0 - jnp.exp(-step_length * density))
        gathered_ref[:, lanes] += weights * two.astype(jnp.float32)
        passed_ref[:, lanes] = passed + density

    @pl.when(sample == pl.num_programs(0) - 1)
    def finish():
        sum_ref[...] = step_length * passed_ref[...]


def compose_kernel(
    share, partner_of, order_ref, gathered_ref, own_ref, *rest
):
    tile_count = order_ref.shape[1]
    others = rest[: tile_count - 1]
    third_ref, keep_ref, send_ref, scale_ref = rest[tile_count - 1 :]
    me = lax.axis_index("depth")
    mine = tile_place(order_ref, me, tile_count)
    before = jnp.zeros_like(own_ref)
    for step in range(1, tile_count):
        ahead = tile_place(order_ref, partner_of(me, step), tile_count) < mine
        before = before + jnp.where(ahead, others[step - 1][...], 0.0)
    scale = jnp.exp(-before)
    scale_ref[...] = scale
    rays = gathered_ref.shape[1]
    half = share // PAIR
    for part in range(rays // share):
        lanes = slice(part * share, (part + 1) * share)
        scaled = (gathered_ref[:, lanes] * scale[:, lanes]).T.astype(jnp.bfloat16)
        features = dot(scaled, third_ref[...]).astype(jnp.bfloat16)
        keep_ref[part * half : (part + 1) * half] = features[:half]
        send_ref[part * half : (part + 1) * half] = features[half:]


def pixel_kernel(slot_rays, arrived_ref, decoder_ref, target_ref, back_ref, stat_ref):
    tile_count, rows, feat_count = arrived_ref.shape
    members = SPP // PAIR
    groups = rows // slot_rays // members
    pixels = groups * slot_rays
    total = arrived_ref[0].astype(jnp.float32)
    for tile in range(1, tile_count):
        total = total + arrived_ref[tile].astype(jnp.float32)
    pieces = []
    for group in range(groups):
        first = group * members * slot_rays
        piece = total[first : first + slot_rays]
        for member in range(1, members):
            start = first + member * slot_rays
            piece = piece + total[start : start + slot_rays]
        pieces.append(piece)
    pixel_mean = jnp.concatenate(pieces, axis=0) / SPP
    mean_square = jnp.mean(pixel_mean * pixel_mean, axis=1, keepdims=True)
    inverse = lax.rsqrt(mean_square + norm_floor)
    normed = pixel_mean * inverse
    decoder = decoder_ref[...]
    row = lax.broadcasted_iota(jnp.int32, (pixels, pixels), 0)
    lane = lax.broadcasted_iota(jnp.int32, (pixels, pixels), 1)
    group_of = lax.div(row, jnp.int32(slot_rays))
    wanted = (row - group_of * slot_rays) * groups + group_of
    pick = (lane == wanted).astype(jnp.float32)
    target = dot_rows(pick, target_ref[...], precision=exact_mode)
    residue = dot_rows(normed, decoder, precision=exact_mode) - target
    stat_ref[0:3] = lax.dot_general(
        residue, normed, lead_lead, preferred_element_type=jnp.float32, precision=exact_mode
    )
    square = jnp.sum(jnp.sum(residue * residue, axis=1, keepdims=True), axis=0, keepdims=True)
    stat_ref[3:4] = jnp.broadcast_to(square, (1, feat_count))
    normed_grad = dot(residue, decoder, precision=exact_mode)
    along = jnp.mean(normed_grad * normed, axis=1, keepdims=True)
    pixel_grad = inverse * (normed_grad - normed * along) / SPP
    spread = []
    for group in range(groups):
        spread += [pixel_grad[group * slot_rays : (group + 1) * slot_rays]] * members
    block = jnp.concatenate(spread, axis=0).astype(jnp.bfloat16)
    for tile in range(tile_count):
        back_ref[tile] = block


def pull_kernel(
    share, near_ref, far_ref, third_ref, gathered_ref, scale_ref, stat_ref, pulled_ref, pack_ref
):
    rays = gathered_ref.shape[1]
    half = share // PAIR
    width = pack_ref.shape[1]
    for part in range(rays // share):
        lanes = slice(part * share, (part + 1) * share)
        rows = slice(part * half, (part + 1) * half)
        ray_grad = jnp.concatenate([near_ref[rows], far_ref[rows]], axis=0)
        pulled = dot_rows(third_ref[...], ray_grad)
        pulled_ref[:, lanes] = pulled
        terms = scale_ref[:, lanes] * jnp.sum(gathered_ref[:, lanes] * pulled, axis=0, keepdims=True)
        line, column = divmod(part * share, width)
        pack_ref[line : line + 1, column : column + share] = terms
    lines = rays // width
    pack_ref[lines : lines + 4] = stat_ref[...]


def weight_kernel(
    share,
    near_ref,
    far_ref,
    two_ref,
    logit_ref,
    gathered_ref,
    scale_ref,
    pulled_ref,
    own_ref,
    third_grad_ref,
    open_ref,
    weight_ref,
    passed_ref,
    behind_ref,
):
    sample = pl.program_id(0)
    rays = gathered_ref.shape[1]
    half = share // PAIR
    width = own_ref.shape[1]

    @pl.when(sample == 0)
    def prepare():
        total = None
        for part in range(rays // share):
            lanes = slice(part * share, (part + 1) * share)
            rows = slice(part * half, (part + 1) * half)
            ray_grad = jnp.concatenate([near_ref[rows], far_ref[rows]], axis=0)
            scaled = (gathered_ref[:, lanes] * scale_ref[:, lanes]).astype(jnp.bfloat16)
            piece = dot(scaled, ray_grad)
            total = piece if total is None else total + piece
            line, column = divmod(part * share, width)
            behind_ref[:, lanes] = own_ref[line : line + 1, column : column + share]
        third_grad_ref[...] = total
        passed_ref[...] = jnp.zeros_like(passed_ref)

    scale = scale_ref[...]
    logits = logit_ref[...]
    density = softplus(logits)
    passed = passed_ref[...]
    through = jnp.exp(-step_length * passed)
    kept = jnp.exp(-step_length * density)
    weights = through * (1.0 - kept)
    pieces = []
    for part in range(rays // share):
        lanes = slice(part * share, (part + 1) * share)
        pieces.append(
            jnp.sum(two_ref[:, lanes].astype(jnp.float32) * pulled_ref[:, lanes], axis=0, keepdims=True)
        )
    weight_grad = scale * jnp.concatenate(pieces, axis=1)
    behind = behind_ref[...] - weights * weight_grad
    behind_ref[...] = behind
    passed_ref[...] = passed + density
    open_ref[...] = through * kept * weight_grad - behind
    weight_ref[...] = weights * scale


def backward_kernel(
    share,
    partner_of,
    order_ref,
    routed_ref,
    one_ref,
    two_ref,
    logit_ref,
    open_ref,
    weight_ref,
    pulled_ref,
    second_ref,
    density_ref,
    *rest,
):
    tile_count = order_ref.shape[1]
    others = rest[: tile_count - 1]
    first_grad_ref, second_grad_ref, density_grad_ref, slope_ref = rest[tile_count - 1 :]
    sample = pl.program_id(0)
    rays = pulled_ref.shape[1]

    @pl.when(sample == 0)
    def prepare():
        me = lax.axis_index("depth")
        mine = tile_place(order_ref, me, tile_count)
        width = others[0].shape[1]
        for part in range(rays // share):
            line, column = divmod(part * share, width)
            slope = jnp.zeros((1, share), jnp.float32)
            for step in range(1, tile_count):
                later = tile_place(order_ref, partner_of(me, step), tile_count) > mine
                terms = others[step - 1][line : line + 1, column : column + share]
                slope = slope - jnp.where(later, terms, 0.0)
            slope_ref[:, part * share : (part + 1) * share] = slope
        first_grad_ref[...] = jnp.zeros_like(first_grad_ref)
        second_grad_ref[...] = jnp.zeros_like(second_grad_ref)
        density_grad_ref[...] = jnp.zeros_like(density_grad_ref)

    logits = logit_ref[...]
    density_grad = step_length * (open_ref[...] + slope_ref[...])
    logit_grad = (density_grad * jax.nn.sigmoid(logits)).astype(jnp.bfloat16)
    weights = weight_ref[...]
    head = density_ref[...].astype(jnp.float32)
    for part in range(rays // share):
        lanes = slice(part * share, (part + 1) * share)
        two = two_ref[:, lanes]
        one = one_ref[:, lanes]
        own_grad = logit_grad[:, lanes]
        wide = weights[:, lanes] * pulled_ref[:, lanes] + head * own_grad.astype(jnp.float32)
        back_two = jnp.where(two > 0, wide, 0.0).astype(jnp.bfloat16)
        second_grad_ref[...] += dot_rows(one, back_two)
        density_grad_ref[...] += dot_rows(own_grad, two)
        back_one = jnp.where(one > 0, dot(second_ref[...], back_two), 0.0).astype(jnp.bfloat16)
        first_grad_ref[...] += dot_rows(routed_ref[:, lanes], back_one)


def whole(shape):
    return pl.BlockSpec(shape, lambda sample: (0,) * len(shape))


def by_sample(rows, rays):
    return pl.BlockSpec((rows, rays), lambda sample: (0, sample))


def one_row(rays):
    return pl.BlockSpec((None, 1, rays), lambda sample: (sample, 0, 0))


def f32(*shape):
    return jax.ShapeDtypeStruct(shape, jnp.float32)


def bf16(*shape):
    return jax.ShapeDtypeStruct(shape, jnp.bfloat16)


def grant(**kwargs):
    return pltpu.CompilerParams(vmem_limit_bytes=vmem_grant, **kwargs)


def body(samples, w_first, w_second, w_third, w_density, decoder, depth_order, ray_slot, target):
    tile_count = lax.axis_size("depth")
    lateral_count = lax.axis_size("lat")
    column_count = lateral_count * PAIR
    inputs = samples[0, 0]
    first, second, third = w_first[0, 0], w_second[0, 0], w_third[0, 0]
    head = w_density[0]
    enc, hid = first.shape
    feat = third.shape[1]
    ray_total = inputs.shape[1] // SAMPLES
    share = ray_total // tile_count
    slot_rays = share // column_count
    half_rays = ray_total // PAIR
    paired = tile_count & (tile_count - 1) == 0

    def partner_of(me, step):
        if paired:
            return jnp.bitwise_xor(me, step)
        return lax.rem(me + tile_count - step, tile_count)

    def from_others(value):
        arrived = []
        for step in range(1, tile_count):
            moves = [
                (tile, tile ^ step if paired else (tile + step) % tile_count)
                for tile in range(tile_count)
            ]
            arrived.append(lax.ppermute(value, "depth", moves))
        return arrived

    swap = [(0, 1), (1, 0)]
    smem = pl.BlockSpec(memory_space=pltpu.SMEM)
    vmem = pl.BlockSpec(memory_space=pltpu.VMEM)

    routed, one, two, logits, gathered, depth_sum = pl.pallas_call(
        functools.partial(forward_kernel, share, slot_rays),
        grid=(SAMPLES,),
        out_shape=(
            bf16(enc, SAMPLES * ray_total),
            bf16(hid, SAMPLES * ray_total),
            bf16(hid, SAMPLES * ray_total),
            f32(SAMPLES, 1, ray_total),
            f32(hid, ray_total),
            f32(1, ray_total),
        ),
        in_specs=[
            by_sample(enc, ray_total),
            whole((1, ray_total)),
            whole((enc, hid)),
            whole((hid, hid)),
            whole((1, hid)),
        ],
        out_specs=(
            by_sample(enc, ray_total),
            by_sample(hid, ray_total),
            by_sample(hid, ray_total),
            one_row(ray_total),
            whole((hid, ray_total)),
            whole((1, ray_total)),
        ),
        scratch_shapes=[
            pltpu.VMEM((tile_count, share, share), jnp.bfloat16),
            pltpu.VMEM((hid, enc), jnp.bfloat16),
            pltpu.VMEM((hid, hid), jnp.bfloat16),
            pltpu.VMEM((1, ray_total), jnp.float32),
        ],
        compiler_params=grant(),
        name="forward_tile",
    )(inputs, ray_slot, first, second, head)

    other_sums = from_others(depth_sum)
    keep, send, scale = pl.pallas_call(
        functools.partial(compose_kernel, share, partner_of),
        out_shape=(bf16(half_rays, feat), bf16(half_rays, feat), f32(1, ray_total)),
        in_specs=[smem] + [vmem] * (tile_count + 2),
        out_specs=(vmem, vmem, vmem),
        compiler_params=grant(),
        name="compose_rays",
    )(depth_order, gathered, depth_sum, *other_sums, third)

    met = lax.ppermute(send, "core", swap)
    joined = (keep.astype(jnp.float32) + met.astype(jnp.float32)).astype(jnp.bfloat16)
    arrived = lax.all_to_all(
        joined.reshape(tile_count * lateral_count, slot_rays, feat),
        ("depth", "lat"),
        split_axis=0,
        concat_axis=0,
        tiled=True,
    )
    back, stats = pl.pallas_call(
        functools.partial(pixel_kernel, slot_rays),
        out_shape=(bf16(tile_count, lateral_count * slot_rays, feat), f32(4, feat)),
        in_specs=[vmem] * 3,
        out_specs=(vmem, vmem),
        compiler_params=grant(),
        name="pixel_loss",
    )(arrived.reshape(tile_count, lateral_count * slot_rays, feat), decoder[0], target[0])

    near = lax.all_to_all(
        back.reshape(tile_count * lateral_count, slot_rays, feat),
        ("depth", "lat"),
        split_axis=0,
        concat_axis=0,
        tiled=True,
    ).reshape(half_rays, feat)
    far = lax.ppermute(near, "core", swap)

    lines = ray_total // feat
    pulled, pack = pl.pallas_call(
        functools.partial(pull_kernel, share),
        out_shape=(f32(hid, ray_total), f32(lines + 4, feat)),
        in_specs=[vmem] * 6,
        out_specs=(vmem, vmem),
        compiler_params=grant(),
        name="pull_rays",
    )(near, far, third, gathered, scale, stats)

    other_packs = from_others(pack)
    third_grad, opened, weights = pl.pallas_call(
        functools.partial(weight_kernel, share),
        grid=(SAMPLES,),
        out_shape=(f32(hid, feat), f32(SAMPLES, 1, ray_total), f32(SAMPLES, 1, ray_total)),
        in_specs=[
            whole((half_rays, feat)),
            whole((half_rays, feat)),
            by_sample(hid, ray_total),
            one_row(ray_total),
            whole((hid, ray_total)),
            whole((1, ray_total)),
            whole((hid, ray_total)),
            whole((lines + 4, feat)),
        ],
        out_specs=(
            whole((hid, feat)),
            one_row(ray_total),
            one_row(ray_total),
        ),
        scratch_shapes=[
            pltpu.VMEM((1, ray_total), jnp.float32),
            pltpu.VMEM((1, ray_total), jnp.float32),
        ],
        compiler_params=grant(),
        name="weight_gradient",
    )(near, far, two, logits, gathered, scale, pulled, pack)

    first_grad, second_grad, density_grad = pl.pallas_call(
        functools.partial(backward_kernel, share, partner_of),
        grid=(SAMPLES,),
        out_shape=(f32(enc, hid), f32(hid, hid), f32(1, hid)),
        in_specs=[
            smem,
            by_sample(enc, ray_total),
            by_sample(hid, ray_total),
            by_sample(hid, ray_total),
            one_row(ray_total),
            one_row(ray_total),
            one_row(ray_total),
            whole((hid, ray_total)),
            whole((hid, hid)),
            whole((hid, 1)),
        ]
        + [whole((lines + 4, feat))] * (tile_count - 1),
        out_specs=(whole((enc, hid)), whole((hid, hid)), whole((1, hid))),
        scratch_shapes=[pltpu.VMEM((1, ray_total), jnp.float32)],
        compiler_params=grant(),
        name="backward_tile",
    )(
        depth_order,
        routed,
        one,
        two,
        logits,
        opened,
        weights,
        pulled,
        second,
        head.reshape(hid, 1),
        *other_packs,
    )

    stat_total = sum(other[lines : lines + 4] for other in other_packs) + pack[lines : lines + 4]
    error = stat_total[3:4, :128]
    error = error + lax.ppermute(error, "core", swap)
    error_total = error
    for step in range(1, lateral_count):
        moves = [(spot, (spot + step) % lateral_count) for spot in range(lateral_count)]
        error_total = error_total + lax.ppermute(error, "lat", moves)
    mean_error = error_total[0, 0] / (3 * column_count * (ray_total // SPP))
    return (
        first_grad[None, None],
        second_grad[None, None],
        third_grad[None, None],
        density_grad[None],
        stat_total[None, :3],
        mean_error,
    )


def solution(mesh):
    shape = mesh.devices.shape
    split = Mesh(
        mesh.devices.reshape(shape[0], shape[1] // PAIR, PAIR), ("depth", "lat", "core")
    )
    lateral = ("lat", "core")
    placed = (
        P("depth", lateral, None, None),
        P("depth", lateral, None, None),
        P("depth", lateral, None, None),
        P("depth", lateral, None, None),
        P("depth", lateral, None),
        P(lateral, None, None),
        P(lateral, None),
        P(lateral, None),
        P(lateral, None, "depth"),
    )
    return jax.shard_map(
        body,
        mesh=split,
        in_specs=placed,
        out_specs=(
            P("depth", lateral, None, None),
            P("depth", lateral, None, None),
            P("depth", lateral, None, None),
            P("depth", lateral, None),
            P(lateral, None, None),
            P(),
        ),
        check_vma=False,
    )
```

```python
import functools

import jax
import jax.numpy as jnp
from jax import lax
from jax.experimental import pallas as pl
from jax.experimental.pallas import tpu as pltpu
from jax.sharding import Mesh
from jax.sharding import PartitionSpec as P

SAMPLES = 8
SPP = 4
PAIR = 2
STEP = 2

step_length = 0.04
norm_floor = 1e-05
exact_mode = lax.Precision.HIGHEST

rows_rows = (((1,), (1,)), ((), ()))
lead_lead = (((0,), (0,)), ((), ()))


def dot(left, right, **how):
    return jnp.dot(left, right, preferred_element_type=jnp.float32, **how)


def dot_rows(left, right, **how):
    return lax.dot_general(left, right, rows_rows, preferred_element_type=jnp.float32, **how)


def softplus(value):
    return jnp.maximum(value, 0.0) + jnp.log1p(jnp.exp(-jnp.abs(value)))


def tile_place(order_ref, tile, tile_count):
    place = jnp.int32(0)
    for position in range(tile_count):
        place = place + jnp.where(order_ref[0, position] == tile, position, 0)
    return place


def forward_kernel(
    share,
    slot_rays,
    stride,
    target_of,
    samples_hbm,
    slot_hbm,
    first_hbm,
    second_hbm,
    density_hbm,
    order_hbm,
    third_hbm,
    *rest,
):
    tile_count = order_hbm.shape[1]
    routed_ref, one_ref, two_ref, logit_ref, gathered_ref, third_ref = rest[:6]
    sum_refs = rest[6 : 5 + tile_count]
    (
        samples_ref,
        slot_ref,
        first_ref,
        second_ref,
        density_ref,
        order_ref,
        route_ref,
        first_turned,
        second_turned,
        small_sem,
        big_sem,
    ) = rest[5 + tile_count :]
    rays = slot_ref.shape[1]
    enc = samples_ref.shape[0]
    total = samples_ref.shape[1]
    samples = total // rays
    shares = rays // share
    small = [
        pltpu.make_async_copy(far, near, small_sem.at[spot])
        for spot, (far, near) in enumerate(
            (
                (slot_hbm, slot_ref),
                (first_hbm, first_ref),
                (second_hbm, second_ref),
                (density_hbm, density_ref),
                (order_hbm, order_ref),
                (third_hbm, third_ref),
            )
        )
    ]
    big = pltpu.make_async_copy(samples_hbm, samples_ref, big_sem.at[0])
    small[0].start()
    big.start()
    for copy in small[1:]:
        copy.start()
    small[0].wait()
    core = lax.axis_index("core")
    target_row = lax.broadcasted_iota(jnp.int32, (share, share), 0)
    for part in range(shares):
        slots = slot_ref[:, part * share : (part + 1) * share]
        owner = lax.div(slots, jnp.int32(slot_rays))
        inside = slots - owner * slot_rays
        lateral = lax.div(owner, jnp.int32(PAIR))
        side = jnp.bitwise_xor(owner - lateral * PAIR, core)
        place = side * (share // PAIR) + lateral * slot_rays + inside
        route_ref[part] = (target_row == place).astype(jnp.float32).astype(jnp.bfloat16)
    for copy in small[1:5]:
        copy.wait()
    first_turned[...] = first_ref[...].T
    second_turned[...] = second_ref[...].T
    big.wait()
    for part in range(shares):
        stacked = jnp.concatenate(
            [
                samples_ref[:, sample * rays + part * share : sample * rays + (part + 1) * share]
                for sample in range(samples)
            ],
            axis=0,
        )
        moved = dot_rows(stacked, route_ref[part]).astype(jnp.bfloat16)
        for sample in range(samples):
            start = sample * rays + part * share
            routed_ref[:, start : start + share] = moved[sample * enc : (sample + 1) * enc]
    weights = []
    passed = jnp.zeros((1, rays), jnp.float32)
    for step in range(total // stride):
        lanes = slice(step * stride, (step + 1) * stride)
        one = jnp.maximum(dot(first_turned[...], routed_ref[:, lanes]), 0.0).astype(jnp.bfloat16)
        one_ref[:, lanes] = one
        two = jnp.maximum(dot(second_turned[...], one), 0.0).astype(jnp.bfloat16)
        two_ref[:, lanes] = two
        logits = dot(density_ref[...], two)
        for part in range(stride // rays):
            sample = step * (stride // rays) + part
            row = logits[:, part * rays : (part + 1) * rays]
            logit_ref[sample : sample + 1] = row
            density = softplus(row)
            weights.append(
                jnp.exp(-step_length * passed) * (1.0 - jnp.exp(-step_length * density))
            )
            passed = passed + density
    depth_sum = step_length * passed
    me = lax.axis_index("depth")
    mine = tile_place(order_ref, me, tile_count)
    for step in range(1, tile_count):
        ahead = mine < tile_place(order_ref, target_of(me, step), tile_count)
        sum_refs[step - 1][...] = jnp.where(ahead, depth_sum, 0.0)
    for start in range(0, rays, 128):
        gathered = None
        for sample in range(samples):
            first = sample * rays + start
            piece = weights[sample][:, start : start + 128] * two_ref[
                :, first : first + 128
            ].astype(jnp.float32)
            gathered = piece if gathered is None else gathered + piece
        gathered_ref[:, start : start + 128] = gathered
    small[5].wait()


def join_kernel(keep_ref, met_ref, joined_ref):
    joined_ref[...] = (
        keep_ref[...].astype(jnp.float32) + met_ref[...].astype(jnp.float32)
    ).astype(jnp.bfloat16)


def compose_kernel(share, gathered_ref, *rest):
    others = rest[:-4]
    third_ref, keep_ref, send_ref, scale_ref = rest[-4:]
    before = others[0][...]
    for other in others[1:]:
        before = before + other[...]
    scale = jnp.exp(-before)
    scale_ref[...] = scale
    rays = gathered_ref.shape[1]
    half = share // PAIR
    for part in range(rays // share):
        lanes = slice(part * share, (part + 1) * share)
        scaled = (gathered_ref[:, lanes] * scale[:, lanes]).T.astype(jnp.bfloat16)
        features = dot(scaled, third_ref[...]).astype(jnp.bfloat16)
        keep_ref[part * half : (part + 1) * half] = features[:half]
        send_ref[part * half : (part + 1) * half] = features[half:]


def pixel_kernel(
    slot_rays, arrived_ref, decoder_ref, target_ref, back_ref, stat_ref, square_ref
):
    tile_count, rows, _ = arrived_ref.shape
    members = SPP // PAIR
    groups = rows // slot_rays // members
    pixels = groups * slot_rays
    total = arrived_ref[0].astype(jnp.float32)
    for tile in range(1, tile_count):
        total = total + arrived_ref[tile].astype(jnp.float32)
    pieces = []
    for group in range(groups):
        first = group * members * slot_rays
        piece = total[first : first + slot_rays]
        for member in range(1, members):
            start = first + member * slot_rays
            piece = piece + total[start : start + slot_rays]
        pieces.append(piece)
    pixel_mean = jnp.concatenate(pieces, axis=0) / SPP
    mean_square = jnp.mean(pixel_mean * pixel_mean, axis=1, keepdims=True)
    inverse = lax.rsqrt(mean_square + norm_floor)
    normed = pixel_mean * inverse
    decoder = decoder_ref[:, 0]
    row = lax.broadcasted_iota(jnp.int32, (pixels, pixels), 0)
    lane = lax.broadcasted_iota(jnp.int32, (pixels, pixels), 1)
    group_of = lax.div(row, jnp.int32(slot_rays))
    wanted = (row - group_of * slot_rays) * groups + group_of
    pick = (lane == wanted).astype(jnp.float32)
    target = dot_rows(pick, target_ref[:, 0], precision=exact_mode)
    residue = dot_rows(normed, decoder, precision=exact_mode) - target
    stat_ref[...] = lax.dot_general(
        residue, normed, lead_lead, preferred_element_type=jnp.float32, precision=exact_mode
    )
    square = jnp.sum(jnp.sum(residue * residue, axis=1, keepdims=True), axis=0, keepdims=True)
    square_ref[...] = jnp.broadcast_to(square, square_ref.shape)
    normed_grad = dot(residue, decoder, precision=exact_mode)
    along = jnp.mean(normed_grad * normed, axis=1, keepdims=True)
    pixel_grad = inverse * (normed_grad - normed * along) / SPP
    spread = []
    for group in range(groups):
        spread += [pixel_grad[group * slot_rays : (group + 1) * slot_rays]] * members
    block = jnp.concatenate(spread, axis=0).astype(jnp.bfloat16)
    for tile in range(tile_count):
        back_ref[tile] = block


def pull_kernel(
    share,
    target_of,
    order_ref,
    near_ref,
    far_ref,
    third_ref,
    gathered_ref,
    scale_ref,
    stat_ref,
    error_ref,
    pulled_ref,
    term_ref,
    *pack_refs,
):
    tile_count = order_ref.shape[1]
    rays = gathered_ref.shape[1]
    half = share // PAIR
    width = stat_ref.shape[1]
    lines = rays // width
    me = lax.axis_index("depth")
    mine = tile_place(order_ref, me, tile_count)
    behind = [
        mine > tile_place(order_ref, target_of(me, step), tile_count)
        for step in range(1, tile_count)
    ]
    for part in range(rays // share):
        lanes = slice(part * share, (part + 1) * share)
        rows = slice(part * half, (part + 1) * half)
        ray_grad = jnp.concatenate([near_ref[rows], far_ref[rows]], axis=0)
        pulled = dot_rows(third_ref[...], ray_grad)
        pulled_ref[:, lanes] = pulled
        terms = scale_ref[:, lanes] * jnp.sum(gathered_ref[:, lanes] * pulled, axis=0, keepdims=True)
        term_ref[:, lanes] = terms
        line, column = divmod(part * share, width)
        for pack_ref, use in zip(pack_refs, behind):
            pack_ref[line : line + 1, column : column + share] = jnp.where(use, terms, 0.0)
    colors = stat_ref.shape[0]
    error = jnp.concatenate([error_ref[...]] * (width // error_ref.shape[1]), axis=1)
    for pack_ref in pack_refs:
        pack_ref[lines : lines + colors] = stat_ref[...]
        pack_ref[lines + colors : lines + colors + 1] = error


def curve_kernel(logit_ref, scale_ref, kept_ref, weight_ref, slope_ref):
    samples, rays = logit_ref.shape
    passed = jnp.zeros((1, rays), jnp.float32)
    for sample in range(samples):
        density = softplus(logit_ref[sample : sample + 1])
        through = jnp.exp(-step_length * passed)
        kept = jnp.exp(-step_length * density)
        kept_ref[sample : sample + 1] = through * kept
        weight_ref[sample : sample + 1] = through * (1.0 - kept) * scale_ref[...]
        passed = passed + density
    slope_ref[...] = step_length * jax.nn.sigmoid(logit_ref[...])


def weight_kernel(
    share,
    near_ref,
    far_ref,
    two_ref,
    gathered_ref,
    scale_ref,
    kept_ref,
    weight_ref,
    pulled_ref,
    term_ref,
    third_grad_ref,
    open_ref,
):
    samples, rays = kept_ref.shape
    half = share // PAIR
    total = None
    for part in range(rays // share):
        lanes = slice(part * share, (part + 1) * share)
        rows = slice(part * half, (part + 1) * half)
        ray_grad = jnp.concatenate([near_ref[rows], far_ref[rows]], axis=0)
        scaled = (gathered_ref[:, lanes] * scale_ref[:, lanes]).astype(jnp.bfloat16)
        piece = dot(scaled, ray_grad)
        total = piece if total is None else total + piece
    third_grad_ref[...] = total
    scale = scale_ref[...]
    behind = term_ref[...]
    for sample in range(samples):
        lanes = slice(sample * rays, (sample + 1) * rays)
        weight_grad = jnp.sum(
            two_ref[:, lanes].astype(jnp.float32) * pulled_ref[...], axis=0, keepdims=True
        )
        behind = behind - weight_ref[sample : sample + 1] * weight_grad
        open_ref[sample : sample + 1] = kept_ref[sample : sample + 1] * scale * weight_grad - behind


def backward_kernel(
    routed_ref,
    one_ref,
    two_ref,
    steep_ref,
    open_ref,
    weight_ref,
    pulled_ref,
    second_ref,
    density_ref,
    stat_ref,
    *rest,
):
    others = rest[:-4]
    first_grad_ref, second_grad_ref, density_grad_ref, decoder_grad_ref = rest[-4:]
    samples, rays = steep_ref.shape
    width = others[0].shape[1]
    lines = rays // width
    colors = stat_ref.shape[0]
    later = others[0][...]
    for other in others[1:]:
        later = later + other[...]
    slope = jnp.concatenate([later[line : line + 1] for line in range(lines)], axis=1)
    for color in range(colors):
        decoder_grad_ref[color] = later[lines + color : lines + color + 1] + stat_ref[color : color + 1]
    logit_grad = ((open_ref[...] - slope) * steep_ref[...]).astype(jnp.bfloat16)
    head = density_ref[...].astype(jnp.float32).T
    first_grad = second_grad = own_grad = None
    for sample in range(samples):
        lanes = slice(sample * rays, (sample + 1) * rays)
        row = logit_grad[sample : sample + 1]
        two = two_ref[:, lanes]
        one = one_ref[:, lanes]
        wide = weight_ref[sample : sample + 1] * pulled_ref[...] + head * row.astype(jnp.float32)
        back_two = jnp.where(two > 0, wide, 0.0).astype(jnp.bfloat16)
        second_piece = dot_rows(one, back_two)
        own_piece = dot_rows(row, two)
        back_one = jnp.where(one > 0, dot(second_ref[...], back_two), 0.0).astype(jnp.bfloat16)
        first_piece = dot_rows(routed_ref[:, lanes], back_one)
        if sample == 0:
            first_grad, second_grad, own_grad = first_piece, second_piece, own_piece
        else:
            first_grad = first_grad + first_piece
            second_grad = second_grad + second_piece
            own_grad = own_grad + own_piece
    first_grad_ref[...] = first_grad
    second_grad_ref[...] = second_grad
    density_grad_ref[...] = own_grad


def f32(*shape):
    return jax.ShapeDtypeStruct(shape, jnp.float32)


def bf16(*shape):
    return jax.ShapeDtypeStruct(shape, jnp.bfloat16)


def grant(size):
    return pltpu.CompilerParams(vmem_limit_bytes=size * 1024 * 1024)


def cost(flops, moved):
    return pl.CostEstimate(flops=flops, bytes_accessed=moved, transcendentals=0)


def body(samples, w_first, w_second, w_third, w_density, decoder, depth_order, ray_slot, target):
    tile_count = lax.axis_size("depth")
    lateral_count = lax.axis_size("lat")
    column_count = lateral_count * PAIR
    inputs = samples[0, 0]
    first, second, third = w_first[0, 0], w_second[0, 0], w_third[0, 0]
    head = w_density[0]
    enc, hid = first.shape
    feat = third.shape[1]
    ray_total = inputs.shape[1] // SAMPLES
    share = ray_total // tile_count
    slot_rays = share // column_count
    half_rays = ray_total // PAIR
    paired = tile_count & (tile_count - 1) == 0
    wide = SAMPLES * ray_total

    def target_of(me, step):
        if paired:
            return jnp.bitwise_xor(me, step)
        return lax.rem(me + step, tile_count)

    def from_others(values):
        arrived = []
        for step in range(1, tile_count):
            moves = [
                (tile, tile ^ step if paired else (tile + step) % tile_count)
                for tile in range(tile_count)
            ]
            arrived.append(lax.ppermute(values[step - 1], "depth", moves))
        return arrived

    swap = [(0, 1), (1, 0)]
    smem = pl.BlockSpec(memory_space=pltpu.SMEM)
    vmem = pl.BlockSpec(memory_space=pltpu.VMEM)
    anywhere = pl.BlockSpec(memory_space=pl.ANY)
    stride = ray_total * STEP

    routed, one, two, logits, gathered, third_near, *sums = pl.pallas_call(
        functools.partial(forward_kernel, share, slot_rays, stride, target_of),
        out_shape=(
            pltpu.VMEM((enc, wide), jnp.bfloat16),
            pltpu.VMEM((hid, wide), jnp.bfloat16),
            pltpu.VMEM((hid, wide), jnp.bfloat16),
            f32(SAMPLES, ray_total),
            pltpu.VMEM((hid, ray_total), jnp.float32),
            pltpu.VMEM((hid, feat), jnp.bfloat16),
        )
        + (f32(1, ray_total),) * (tile_count - 1),
        in_specs=[anywhere] * 7,
        out_specs=(vmem,) * (tile_count + 5),
        scratch_shapes=[
            pltpu.VMEM((enc, wide), jnp.bfloat16),
            pltpu.VMEM((1, ray_total), jnp.int32),
            pltpu.VMEM((enc, hid), jnp.bfloat16),
            pltpu.VMEM((hid, hid), jnp.bfloat16),
            pltpu.VMEM((1, hid), jnp.bfloat16),
            pltpu.SMEM((1, tile_count), jnp.int32),
            pltpu.VMEM((tile_count, share, share), jnp.bfloat16),
            pltpu.VMEM((hid, enc), jnp.bfloat16),
            pltpu.VMEM((hid, hid), jnp.bfloat16),
            pltpu.SemaphoreType.DMA((6,)),
            pltpu.SemaphoreType.DMA((1,)),
        ],
        compiler_params=grant(32),
        name="forward_tile",
    )(
        *[
            pltpu.with_memory_space_constraint(value, pltpu.HBM)
            for value in (inputs, ray_slot, first, second, head, depth_order, third)
        ]
    )

    other_sums = from_others(sums)
    routed, one, two, gathered, third_near = (
        pltpu.with_memory_space_constraint(value, pltpu.VMEM)
        for value in (routed, one, two, gathered, third_near)
    )
    keep, send, scale = pl.pallas_call(
        functools.partial(compose_kernel, share),
        out_shape=(bf16(half_rays, feat), bf16(half_rays, feat), f32(1, ray_total)),
        in_specs=[vmem] * (tile_count + 1),
        out_specs=(vmem, vmem, vmem),
        compiler_params=grant(16),
        cost_estimate=cost(0, 20 * feat * half_rays),
        name="compose_rays",
    )(gathered, *other_sums, third_near)

    met = lax.ppermute(send, "core", swap)
    joined = pl.pallas_call(
        join_kernel,
        out_shape=bf16(half_rays, feat),
        in_specs=[vmem] * 2,
        out_specs=vmem,
        compiler_params=grant(16),
        name="join_pair",
    )(keep, met)
    arrived = lax.all_to_all(
        joined.reshape(tile_count * lateral_count, slot_rays, feat),
        ("depth", "lat"),
        split_axis=0,
        concat_axis=0,
        tiled=True,
    )
    decoder_lines = jnp.transpose(decoder, (1, 0, 2))
    target_lines = jnp.transpose(target, (1, 0, 2))
    back, stats, error = pl.pallas_call(
        functools.partial(pixel_kernel, slot_rays),
        out_shape=(
            bf16(tile_count, lateral_count * slot_rays, feat),
            f32(decoder.shape[1], feat),
            f32(1, 128),
        ),
        in_specs=[vmem] * 3,
        out_specs=(vmem,) * 3,
        compiler_params=grant(16),
        cost_estimate=cost(0, 200 * feat * half_rays),
        name="pixel_loss",
    )(arrived.reshape(tile_count, lateral_count * slot_rays, feat), decoder_lines, target_lines)

    near = lax.all_to_all(
        back.reshape(tile_count * lateral_count, slot_rays, feat),
        ("depth", "lat"),
        split_axis=0,
        concat_axis=0,
        tiled=True,
    ).reshape(half_rays, feat)
    far = lax.ppermute(near, "core", swap)

    error = error + lax.ppermute(error, "core", swap)
    kept, weights, steep = pl.pallas_call(
        curve_kernel,
        out_shape=(f32(SAMPLES, ray_total),) * 3,
        in_specs=[vmem] * 2,
        out_specs=(vmem,) * 3,
        compiler_params=grant(16),
        cost_estimate=cost(0, 16 * hid * ray_total),
        name="ray_curves",
    )(logits, scale)

    lines = ray_total // feat
    pack_rows = lines + decoder.shape[1] + 1
    pack_rows = lines + decoder.shape[1] + 1
    pulled, terms, *packs = pl.pallas_call(
        functools.partial(pull_kernel, share, target_of),
        out_shape=(f32(hid, ray_total), f32(1, ray_total))
        + (f32(pack_rows, feat),) * (tile_count - 1),
        in_specs=[smem] + [vmem] * 7,
        out_specs=(vmem,) * (tile_count + 1),
        compiler_params=grant(16),
        cost_estimate=cost(0, 50 * feat * half_rays),
        name="pull_rays",
    )(depth_order, near, far, third_near, gathered, scale, stats, error)

    other_packs = from_others(packs)
    third_grad, opened = pl.pallas_call(
        functools.partial(weight_kernel, share),
        out_shape=(f32(hid, feat), f32(SAMPLES, ray_total)),
        in_specs=[vmem] * 9,
        out_specs=(vmem,) * 2,
        compiler_params=grant(16),
        cost_estimate=cost(4 * hid * wide, 3 * hid * wide),
        name="weight_gradient",
    )(near, far, two, gathered, scale, kept, weights, pulled, terms)

    first_grad, second_grad, density_grad, decoder_grad = pl.pallas_call(
        backward_kernel,
        out_shape=(
            f32(enc, hid),
            f32(hid, hid),
            f32(1, hid),
            f32(decoder.shape[1], 1, feat),
        ),
        in_specs=[vmem] * (9 + tile_count),
        out_specs=(vmem,) * 4,
        compiler_params=grant(20),
        cost_estimate=cost(6 * hid * hid * wide, 10 * hid * wide),
        name="backward_tile",
    )(
        routed,
        one,
        two,
        steep,
        opened,
        weights,
        pulled,
        second,
        head,
        stats,
        *other_packs,
    )

    for other in other_packs:
        error = error + other[pack_rows - 1 : pack_rows, :128]
    total = error
    for step in range(1, lateral_count):
        moves = [(spot, (spot + step) % lateral_count) for spot in range(lateral_count)]
        total = total + lax.ppermute(error, "lat", moves)
    mean_error = total / (decoder.shape[1] * column_count * (ray_total // SPP))
    return (
        first_grad[None, None],
        second_grad[None, None],
        third_grad[None, None],
        density_grad[None],
        jnp.transpose(decoder_grad, (1, 0, 2)),
        mean_error[0, 0],
    )


def solution(mesh):
    shape = mesh.devices.shape
    split = Mesh(
        mesh.devices.reshape(shape[0], shape[1] // PAIR, PAIR), ("depth", "lat", "core")
    )
    lateral = ("lat", "core")
    placed = (
        P("depth", lateral, None, None),
        P("depth", lateral, None, None),
        P("depth", lateral, None, None),
        P("depth", lateral, None, None),
        P("depth", lateral, None),
        P(lateral, None, None),
        P(lateral, None),
        P(lateral, None),
        P(lateral, None, "depth"),
    )
    return jax.shard_map(
        body,
        mesh=split,
        in_specs=placed,
        out_specs=(
            P("depth", lateral, None, None),
            P("depth", lateral, None, None),
            P("depth", lateral, None, None),
            P("depth", lateral, None),
            P(lateral, None, None),
            P(),
        ),
        check_vma=False,
    )
```

```python
import functools

import jax
import jax.numpy as jnp
from jax import lax
from jax.experimental import pallas as pl
from jax.experimental.pallas import tpu as pltpu
from jax.sharding import Mesh
from jax.sharding import PartitionSpec as P

SAMPLES = 8
SPP = 4
PAIR = 2
STEP = 2
TILE = 8

step_length = 0.04
norm_floor = 1e-05
exact_mode = lax.Precision.HIGHEST

rows_rows = (((1,), (1,)), ((), ()))
lead_lead = (((0,), (0,)), ((), ()))


def dot(left, right, **how):
    return jnp.dot(left, right, preferred_element_type=jnp.float32, **how)


def dot_rows(left, right, **how):
    return lax.dot_general(left, right, rows_rows, preferred_element_type=jnp.float32, **how)


def softplus(value):
    return jnp.maximum(value, 0.0) + jnp.log1p(jnp.exp(-jnp.abs(value)))


def tile_place(order_ref, tile, tile_count):
    place = jnp.int32(0)
    for position in range(tile_count):
        place = place + jnp.where(order_ref[0, position] == tile, position, 0)
    return place


def forward_kernel(
    share,
    slot_rays,
    stride,
    target_of,
    samples_hbm,
    slot_hbm,
    first_hbm,
    second_hbm,
    density_hbm,
    order_hbm,
    third_hbm,
    *rest,
):
    tile_count = order_hbm.shape[1]
    routed_ref, one_ref, two_ref, logit_ref, behind_ref, third_ref = rest[:6]
    sum_refs = rest[6 : 5 + tile_count]
    (
        samples_ref,
        slot_ref,
        first_ref,
        second_ref,
        density_ref,
        order_ref,
        route_ref,
        first_turned,
        second_turned,
        small_sem,
        big_sem,
    ) = rest[5 + tile_count :]
    rays = slot_ref.shape[1]
    enc = samples_ref.shape[0]
    total = samples_ref.shape[1]
    samples = total // rays
    shares = rays // share
    small = [
        pltpu.make_async_copy(far, near, small_sem.at[spot])
        for spot, (far, near) in enumerate(
            (
                (slot_hbm, slot_ref),
                (first_hbm, first_ref),
                (second_hbm, second_ref),
                (density_hbm, density_ref),
                (order_hbm, order_ref),
                (third_hbm, third_ref),
            )
        )
    ]
    big = pltpu.make_async_copy(samples_hbm, samples_ref, big_sem.at[0])
    small[0].start()
    big.start()
    for copy in small[1:]:
        copy.start()
    small[0].wait()
    core = lax.axis_index("core")
    target_row = lax.broadcasted_iota(jnp.int32, (share, share), 0)
    for part in range(shares):
        slots = slot_ref[:, part * share : (part + 1) * share]
        owner = lax.div(slots, jnp.int32(slot_rays))
        inside = slots - owner * slot_rays
        lateral = lax.div(owner, jnp.int32(PAIR))
        side = jnp.bitwise_xor(owner - lateral * PAIR, core)
        place = side * (share // PAIR) + lateral * slot_rays + inside
        route_ref[part] = (target_row == place).astype(jnp.float32).astype(jnp.bfloat16)
    for copy in small[1:5]:
        copy.wait()
    first_turned[...] = first_ref[...].T
    second_turned[...] = second_ref[...].T
    big.wait()
    for part in range(shares):
        stacked = jnp.concatenate(
            [
                samples_ref[:, sample * rays + part * share : sample * rays + (part + 1) * share]
                for sample in range(samples)
            ],
            axis=0,
        )
        moved = dot_rows(stacked, route_ref[part]).astype(jnp.bfloat16)
        for sample in range(samples):
            start = sample * rays + part * share
            routed_ref[:, start : start + share] = moved[sample * enc : (sample + 1) * enc]
    passed = jnp.zeros((1, rays), jnp.float32)
    for step in range(total // stride):
        lanes = slice(step * stride, (step + 1) * stride)
        one = jnp.maximum(dot(first_turned[...], routed_ref[:, lanes]), 0.0).astype(jnp.bfloat16)
        one_ref[:, lanes] = one
        two = jnp.maximum(dot(second_turned[...], one), 0.0).astype(jnp.bfloat16)
        two_ref[:, lanes] = two
        logits = dot(density_ref[...], two)
        for part in range(stride // rays):
            sample = step * (stride // rays) + part
            row = logits[:, part * rays : (part + 1) * rays]
            logit_ref[sample : sample + 1] = row
            density = softplus(row)
            passed = passed + density
    depth_sum = step_length * passed
    me = lax.axis_index("depth")
    mine = tile_place(order_ref, me, tile_count)
    for step in range(1, tile_count):
        ahead = mine < tile_place(order_ref, target_of(me, step), tile_count)
        sum_refs[step - 1][...] = jnp.where(ahead, depth_sum, 0.0)
        behind_ref[step - 1 : step] = jnp.where(
            ahead, jnp.zeros((1, 128), jnp.float32), jnp.ones((1, 128), jnp.float32)
        )
    small[5].wait()


def join_kernel(keep_ref, met_ref, joined_ref):
    joined_ref[...] = (
        keep_ref[...].astype(jnp.float32) + met_ref[...].astype(jnp.float32)
    ).astype(jnp.bfloat16)


def gather_kernel(two_ref, logit_ref, gathered_ref):
    samples, rays = logit_ref.shape
    passed = jnp.zeros((1, rays), jnp.float32)
    weights = []
    for sample in range(samples):
        density = softplus(logit_ref[sample : sample + 1])
        weights.append(jnp.exp(-step_length * passed) * (1.0 - jnp.exp(-step_length * density)))
        passed = passed + density
    for start in range(0, rays, 128):
        gathered = None
        for sample in range(samples):
            first = sample * rays + start
            piece = weights[sample][:, start : start + 128] * two_ref[
                :, first : first + 128
            ].astype(jnp.float32)
            gathered = piece if gathered is None else gathered + piece
        gathered_ref[:, start : start + 128] = gathered


def compose_kernel(share, gathered_ref, *rest):
    others = rest[:-4]
    third_ref, keep_ref, send_ref, scale_ref = rest[-4:]
    before = others[0][...]
    for other in others[1:]:
        before = before + other[...]
    scale = jnp.exp(-before)
    scale_ref[...] = scale
    rays = gathered_ref.shape[1]
    half = share // PAIR
    for part in range(rays // share):
        lanes = slice(part * share, (part + 1) * share)
        scaled = (gathered_ref[:, lanes] * scale[:, lanes]).T.astype(jnp.bfloat16)
        features = dot(scaled, third_ref[...]).astype(jnp.bfloat16)
        keep_ref[part * half : (part + 1) * half] = features[:half]
        send_ref[part * half : (part + 1) * half] = features[half:]


def pixel_kernel(
    slot_rays, packed, arrived_ref, decoder_ref, target_ref, back_ref, stat_ref, *square_refs
):
    tile_count, rows, _ = arrived_ref.shape
    members = SPP // PAIR
    groups = rows // slot_rays // members
    pixels = groups * slot_rays
    total = arrived_ref[0].astype(jnp.float32)
    for tile in range(1, tile_count):
        total = total + arrived_ref[tile].astype(jnp.float32)
    pieces = []
    for group in range(groups):
        first = group * members * slot_rays
        piece = total[first : first + slot_rays]
        for member in range(1, members):
            start = first + member * slot_rays
            piece = piece + total[start : start + slot_rays]
        pieces.append(piece)
    pixel_mean = jnp.concatenate(pieces, axis=0) / SPP
    mean_square = jnp.mean(pixel_mean * pixel_mean, axis=1, keepdims=True)
    inverse = lax.rsqrt(mean_square + norm_floor)
    normed = pixel_mean * inverse
    decoder = decoder_ref[:, 0]
    row = lax.broadcasted_iota(jnp.int32, (pixels, pixels), 0)
    lane = lax.broadcasted_iota(jnp.int32, (pixels, pixels), 1)
    group_of = lax.div(row, jnp.int32(slot_rays))
    wanted = (row - group_of * slot_rays) * groups + group_of
    pick = (lane == wanted).astype(jnp.float32)
    target = dot_rows(pick, target_ref[:, 0], precision=exact_mode)
    residue = dot_rows(normed, decoder, precision=exact_mode) - target
    stat_ref[...] = lax.dot_general(
        residue, normed, lead_lead, preferred_element_type=jnp.float32, precision=exact_mode
    )
    square = jnp.sum(jnp.sum(residue * residue, axis=1, keepdims=True), axis=0, keepdims=True)
    for square_ref in square_refs:
        square_ref[...] = jnp.broadcast_to(square, square_ref.shape)
    normed_grad = dot(residue, decoder, precision=exact_mode)
    along = jnp.mean(normed_grad * normed, axis=1, keepdims=True)
    pixel_grad = inverse * (normed_grad - normed * along) / SPP
    spread = []
    for group in range(groups):
        spread += [pixel_grad[group * slot_rays : (group + 1) * slot_rays]] * members
    if not packed:
        block = jnp.concatenate(spread, axis=0).astype(jnp.bfloat16)
        for tile in range(tile_count):
            back_ref[tile] = block
        return
    near = jnp.broadcast_to(square, (1, 128))
    split = []
    for _ in range(3):
        split.append(near.astype(jnp.bfloat16).astype(jnp.float32))
        near = near - split[-1]
    split.append(jnp.zeros((TILE - 3, 128), jnp.float32))
    extra = jnp.concatenate(split, axis=0).astype(jnp.bfloat16)
    height = pixel_grad.shape[1] // 128 * slot_rays + TILE
    for spot, piece in enumerate(spread):
        base = spot * height
        narrow = piece.astype(jnp.bfloat16)
        for tile in range(tile_count):
            for column in range(pixel_grad.shape[1] // 128):
                start = base + column * slot_rays
                back_ref[tile, start : start + slot_rays] = narrow[
                    :, column * 128 : (column + 1) * 128
                ]
            back_ref[tile, base + height - TILE : base + height] = extra


def half_share(ref, part, slot_rays, blocks, feat, packed):
    if not packed:
        half = slot_rays * blocks
        return ref[part * half : (part + 1) * half]
    height = feat // 128 * slot_rays + TILE
    pieces = []
    for block in range(part * blocks, (part + 1) * blocks):
        base = block * height
        pieces.append(
            jnp.concatenate(
                [
                    ref[base + column * slot_rays : base + (column + 1) * slot_rays]
                    for column in range(feat // 128)
                ],
                axis=1,
            )
        )
    return jnp.concatenate(pieces, axis=0)


def pull(third_ref, gathered_ref, scale_ref, ray_grad, side, share):
    rays = gathered_ref.shape[1]
    half = share // PAIR
    starts = range(side * half, rays, share)
    gathered = jnp.concatenate([gathered_ref[:, at : at + half] for at in starts], axis=1)
    scale = jnp.concatenate([scale_ref[:, at : at + half] for at in starts], axis=1)
    scaled = gathered * scale
    pulled = dot_rows(third_ref[...], ray_grad)
    return pulled, scaled, jnp.sum(scaled * pulled, axis=0, keepdims=True)


def near_kernel(
    share,
    rays_of,
    near_ref,
    third_ref,
    gathered_ref,
    scale_ref,
    pulled_ref,
    term_ref,
    partial_ref,
):
    shares = gathered_ref.shape[1] // share
    ray_grad = jnp.concatenate([rays_of(near_ref, part) for part in range(shares)], axis=0)
    pulled, scaled, terms = pull(third_ref, gathered_ref, scale_ref, ray_grad, 0, share)
    pulled_ref[...] = pulled
    term_ref[...] = terms
    partial_ref[...] = dot(scaled.astype(jnp.bfloat16), ray_grad)


def far_kernel(
    share,
    rays_of,
    behind_ref,
    far_ref,
    third_ref,
    gathered_ref,
    scale_ref,
    stat_ref,
    near_pulled_ref,
    near_term_ref,
    pulled_ref,
    term_ref,
    ray_grad_ref,
    scaled_ref,
    *pack_refs,
):
    rays = gathered_ref.shape[1]
    width = stat_ref.shape[1]
    lines = rays // width
    half = share // PAIR
    ray_grad = jnp.concatenate([rays_of(far_ref, part) for part in range(rays // share)], axis=0)
    ray_grad_ref[...] = ray_grad
    pulled, scaled, terms = pull(third_ref, gathered_ref, scale_ref, ray_grad, 1, share)
    scaled_ref[...] = scaled.astype(jnp.bfloat16)
    pieces = []
    for part in range(rays // share):
        lanes = slice(part * share, (part + 1) * share)
        own = slice(part * half, (part + 1) * half)
        pulled_ref[:, lanes] = jnp.concatenate([near_pulled_ref[:, own], pulled[:, own]], axis=1)
        pieces += [near_term_ref[:, own], terms[:, own]]
    terms = jnp.concatenate(pieces, axis=1)
    term_ref[...] = terms
    for step, pack_ref in enumerate(pack_refs):
        for line in range(lines):
            row = terms[:, line * width : (line + 1) * width]
            use = jnp.concatenate([behind_ref[step : step + 1]] * (width // 128), axis=1)
            pack_ref[line : line + 1] = jnp.where(use > 0.0, row, 0.0)
        pack_ref[lines : lines + stat_ref.shape[0]] = stat_ref[...]


def curve_kernel(logit_ref, scale_ref, kept_ref, weight_ref, slope_ref):
    samples, rays = logit_ref.shape
    passed = jnp.zeros((1, rays), jnp.float32)
    for sample in range(samples):
        density = softplus(logit_ref[sample : sample + 1])
        through = jnp.exp(-step_length * passed)
        kept = jnp.exp(-step_length * density)
        kept_ref[sample : sample + 1] = through * kept
        weight_ref[sample : sample + 1] = through * (1.0 - kept) * scale_ref[...]
        passed = passed + density
    slope_ref[...] = step_length * jax.nn.sigmoid(logit_ref[...])


def weight_kernel(two_ref, scale_ref, kept_ref, weight_ref, pulled_ref, term_ref, open_ref):
    samples, rays = kept_ref.shape
    scale = scale_ref[...]
    behind = term_ref[...]
    for sample in range(samples):
        lanes = slice(sample * rays, (sample + 1) * rays)
        weight_grad = jnp.sum(
            two_ref[:, lanes].astype(jnp.float32) * pulled_ref[...], axis=0, keepdims=True
        )
        behind = behind - weight_ref[sample : sample + 1] * weight_grad
        open_ref[sample : sample + 1] = kept_ref[sample : sample + 1] * scale * weight_grad - behind


def backward_kernel(
    share,
    entries,
    height,
    routed_ref,
    one_ref,
    two_ref,
    steep_ref,
    open_ref,
    weight_ref,
    pulled_ref,
    second_ref,
    density_ref,
    stat_ref,
    near_ref,
    far_ref,
    far_rays_ref,
    far_scaled_ref,
    partial_ref,
    *rest,
):
    outputs = 5 + int(height > 0)
    others = rest[: -2 * outputs - 3]
    result_hbms = rest[-2 * outputs - 3 : -outputs - 3]
    back_two_ref, back_one_ref = rest[-outputs - 3 : -outputs - 1]
    results = rest[-outputs - 1 : -1]
    first_grad_ref, second_grad_ref, third_grad_ref, density_grad_ref, decoder_grad_ref = results[:5]
    sem = rest[-1]
    leaving = [
        pltpu.make_async_copy(near, far, sem.at[spot])
        for spot, (near, far) in enumerate(zip(results, result_hbms))
    ]
    third_grad_ref[...] = partial_ref[...] + dot(far_scaled_ref[...], far_rays_ref[...])
    leaving[2].start()
    for mean_ref in results[5:]:
        error = None
        for ref in (near_ref, far_ref):
            for base in range(height - TILE, ref.shape[0], height):
                piece = ref[base : base + TILE].astype(jnp.float32)
                error = piece if error is None else error + piece
        mean_ref[...] = jnp.sum(error, axis=0, keepdims=True) / entries
        leaving[5].start()
    samples, rays = steep_ref.shape
    width = others[0].shape[1]
    lines = rays // width
    colors = stat_ref.shape[0]
    later = others[0][...]
    for other in others[1:]:
        later = later + other[...]
    slope = jnp.concatenate([later[line : line + 1] for line in range(lines)], axis=1)
    for color in range(colors):
        total = later[lines + color : lines + color + 1]
        decoder_grad_ref[color] = total + stat_ref[color : color + 1]
    leaving[4].start()
    logit_grad = ((open_ref[...] - slope) * steep_ref[...]).astype(jnp.bfloat16)
    head = density_ref[...].astype(jnp.float32).T
    first_grad = second_grad = own_grad = None
    for sample in range(samples):
        lanes = slice(sample * rays, (sample + 1) * rays)
        row = logit_grad[sample : sample + 1].astype(jnp.float32)
        two = two_ref[:, lanes]
        weighted = weight_ref[sample : sample + 1] * pulled_ref[...] + head * row
        back_two_ref[...] = jnp.where(two > 0, weighted.astype(jnp.bfloat16), jnp.zeros_like(two))
        piece = dot_rows(one_ref[:, lanes], back_two_ref[...])
        second_grad = piece if second_grad is None else second_grad + piece
        if sample == samples - 1:
            second_grad_ref[...] = second_grad
            leaving[1].start()
        for start in range(0, rays, 128):
            window = slice(sample * rays + start, sample * rays + start + 128)
            piece = two_ref[:, window].astype(jnp.float32) * row[:, start : start + 128]
            own_grad = piece if own_grad is None else own_grad + piece
        for start in range(0, rays, share):
            one = one_ref[:, sample * rays + start : sample * rays + start + share]
            back = dot(second_ref[...], back_two_ref[:, start : start + share])
            back_one_ref[:, start : start + share] = jnp.where(
                one > 0, back.astype(jnp.bfloat16), jnp.zeros_like(one)
            )
        piece = dot_rows(routed_ref[:, lanes], back_one_ref[...])
        first_grad = piece if first_grad is None else first_grad + piece
    first_grad_ref[...] = first_grad
    leaving[0].start()
    density_grad_ref[...] = jnp.sum(own_grad, axis=1, keepdims=True).T
    leaving[3].start()
    for copy in leaving:
        copy.wait()


def f32(*shape):
    return jax.ShapeDtypeStruct(shape, jnp.float32)


def bf16(*shape):
    return jax.ShapeDtypeStruct(shape, jnp.bfloat16)


def grant(size):
    return pltpu.CompilerParams(vmem_limit_bytes=size * 1024 * 1024)


def cost(flops, moved):
    return pl.CostEstimate(flops=flops, bytes_accessed=moved, transcendentals=0)


def body(samples, w_first, w_second, w_third, w_density, decoder, depth_order, ray_slot, target):
    tile_count = lax.axis_size("depth")
    lateral_count = lax.axis_size("lat")
    column_count = lateral_count * PAIR
    inputs = samples[0, 0]
    first, second, third = w_first[0, 0], w_second[0, 0], w_third[0, 0]
    head = w_density[0]
    enc, hid = first.shape
    feat = third.shape[1]
    ray_total = inputs.shape[1] // SAMPLES
    share = ray_total // tile_count
    slot_rays = share // column_count
    half_rays = ray_total // PAIR
    paired = tile_count & (tile_count - 1) == 0
    wide = SAMPLES * ray_total

    def target_of(me, step):
        if paired:
            return jnp.bitwise_xor(me, step)
        return lax.rem(me + step, tile_count)

    def from_others(values):
        arrived = []
        for step in reversed(range(1, tile_count)):
            moves = [
                (tile, tile ^ step if paired else (tile + step) % tile_count)
                for tile in range(tile_count)
            ]
            arrived.append(lax.ppermute(values[step - 1], "depth", moves))
        return arrived

    swap = [(0, 1), (1, 0)]
    vmem = pl.BlockSpec(memory_space=pltpu.VMEM)
    anywhere = pl.BlockSpec(memory_space=pl.ANY)
    stride = ray_total * STEP

    routed, one, two, logits, behind, third_near, *sums = pl.pallas_call(
        functools.partial(forward_kernel, share, slot_rays, stride, target_of),
        out_shape=(
            pltpu.VMEM((enc, wide), jnp.bfloat16),
            pltpu.VMEM((hid, wide), jnp.bfloat16),
            pltpu.VMEM((hid, wide), jnp.bfloat16),
            f32(SAMPLES, ray_total),
            f32(tile_count - 1, 128),
            pltpu.VMEM((hid, feat), jnp.bfloat16),
        )
        + (f32(1, ray_total),) * (tile_count - 1),
        in_specs=[anywhere] * 7,
        out_specs=(vmem,) * (tile_count + 5),
        scratch_shapes=[
            pltpu.VMEM((enc, wide), jnp.bfloat16),
            pltpu.VMEM((1, ray_total), jnp.int32),
            pltpu.VMEM((enc, hid), jnp.bfloat16),
            pltpu.VMEM((hid, hid), jnp.bfloat16),
            pltpu.VMEM((1, hid), jnp.bfloat16),
            pltpu.SMEM((1, tile_count), jnp.int32),
            pltpu.VMEM((tile_count, share, share), jnp.bfloat16),
            pltpu.VMEM((hid, enc), jnp.bfloat16),
            pltpu.VMEM((hid, hid), jnp.bfloat16),
            pltpu.SemaphoreType.DMA((6,)),
            pltpu.SemaphoreType.DMA((1,)),
        ],
        compiler_params=grant(32),
        name="forward_tile",
    )(
        *[
            pltpu.with_memory_space_constraint(value, pltpu.HBM)
            for value in (inputs, ray_slot, first, second, head, depth_order, third)
        ]
    )

    other_sums = from_others(sums)
    routed, one, two, third_near = (
        pltpu.with_memory_space_constraint(value, pltpu.VMEM)
        for value in (routed, one, two, third_near)
    )
    gathered = pl.pallas_call(
        gather_kernel,
        out_shape=f32(hid, ray_total),
        in_specs=[vmem] * 2,
        out_specs=vmem,
        compiler_params=grant(16),
        cost_estimate=cost(4 * hid * wide, 3 * hid * wide),
        name="gather_samples",
    )(two, logits)
    keep, send, scale = pl.pallas_call(
        functools.partial(compose_kernel, share),
        out_shape=(bf16(half_rays, feat), bf16(half_rays, feat), f32(1, ray_total)),
        in_specs=[vmem] * (tile_count + 1),
        out_specs=(vmem, vmem, vmem),
        compiler_params=grant(16),
        cost_estimate=cost(0, 20 * feat * half_rays),
        name="compose_rays",
    )(gathered, *other_sums, third_near)

    met = lax.ppermute(send, "core", swap)
    joined = pl.pallas_call(
        join_kernel,
        out_shape=bf16(half_rays, feat),
        in_specs=[vmem] * 2,
        out_specs=vmem,
        compiler_params=grant(16),
        name="join_pair",
    )(keep, met)
    arrived = lax.all_to_all(
        joined.reshape(tile_count * lateral_count, slot_rays, feat),
        ("depth", "lat"),
        split_axis=0,
        concat_axis=0,
        tiled=True,
    )
    packed = slot_rays % 16 == 0
    height = feat // 128 * slot_rays + TILE if packed else slot_rays
    width = 128 if packed else feat
    rays_of = functools.partial(
        half_share, slot_rays=slot_rays, blocks=lateral_count, feat=feat, packed=packed
    )
    entries = decoder.shape[1] * column_count * (ray_total // SPP)
    decoder_lines = jnp.transpose(decoder, (1, 0, 2))
    target_lines = jnp.transpose(target, (1, 0, 2))
    back, stats, *error = pl.pallas_call(
        functools.partial(pixel_kernel, slot_rays, packed),
        out_shape=(
            bf16(tile_count, lateral_count * height, width),
            f32(decoder.shape[1], feat),
        )
        + (f32(1, 128),) * int(not packed),
        in_specs=[vmem] * 3,
        out_specs=(vmem,) * (2 + int(not packed)),
        compiler_params=grant(16),
        cost_estimate=cost(0, 200 * feat * half_rays),
        name="pixel_loss",
    )(arrived.reshape(tile_count, lateral_count * slot_rays, feat), decoder_lines, target_lines)

    near = lax.all_to_all(
        back.reshape(tile_count * lateral_count, height, width),
        ("depth", "lat"),
        split_axis=0,
        concat_axis=0,
        tiled=True,
    ).reshape(tile_count * lateral_count * height, width)
    far = lax.ppermute(near, "core", swap)

    kept, weights, steep = pl.pallas_call(
        curve_kernel,
        out_shape=(f32(SAMPLES, ray_total),) * 3,
        in_specs=[vmem] * 2,
        out_specs=(vmem,) * 3,
        compiler_params=grant(16),
        cost_estimate=cost(0, 16 * hid * ray_total),
        name="ray_curves",
    )(logits, scale)

    lines = ray_total // feat
    pack_rows = lines + decoder.shape[1]
    pack_rows = lines + decoder.shape[1]
    near_pulled, near_terms, partial = pl.pallas_call(
        functools.partial(near_kernel, share, rays_of),
        out_shape=(f32(hid, half_rays), f32(1, half_rays), f32(hid, feat)),
        in_specs=[vmem] * 4,
        out_specs=(vmem,) * 3,
        compiler_params=grant(16),
        cost_estimate=cost(4 * hid * feat * half_rays, 8 * hid * ray_total),
        name="near_rays",
    )(near, third_near, gathered, scale)
    pulled, terms, far_rays, far_scaled, *packs = pl.pallas_call(
        functools.partial(far_kernel, share, rays_of),
        out_shape=(f32(hid, ray_total), f32(1, ray_total), bf16(half_rays, feat), bf16(hid, half_rays))
        + (f32(pack_rows, feat),) * (tile_count - 1),
        in_specs=[vmem] * 8,
        out_specs=(vmem,) * (3 + tile_count),
        compiler_params=grant(16),
        cost_estimate=cost(0, 50 * feat * half_rays),
        name="far_rays",
    )(behind, far, third_near, gathered, scale, stats, near_pulled, near_terms)

    other_packs = from_others(packs)
    opened = pl.pallas_call(
        weight_kernel,
        out_shape=f32(SAMPLES, ray_total),
        in_specs=[vmem] * 6,
        out_specs=vmem,
        compiler_params=grant(16),
        cost_estimate=cost(0, 3 * hid * wide),
        name="weight_gradient",
    )(two, scale, kept, weights, pulled, terms)

    results = [
        (enc, hid),
        (hid, hid),
        (hid, feat),
        (1, hid),
        (decoder.shape[1], 1, feat),
    ] + [(1, 128)] * int(packed)
    first_grad, second_grad, third_grad, density_grad, decoder_grad, *mean = pl.pallas_call(
        functools.partial(backward_kernel, share, entries, height if packed else 0),
        out_shape=tuple(f32(*shape) for shape in results),
        in_specs=[vmem] * (14 + tile_count),
        out_specs=(anywhere,) * len(results),
        scratch_shapes=[pltpu.VMEM((hid, ray_total), jnp.bfloat16)] * 2
        + [pltpu.VMEM(shape, jnp.float32) for shape in results]
        + [pltpu.SemaphoreType.DMA((len(results),))],
        compiler_params=grant(20),
        cost_estimate=cost(6 * hid * hid * wide, 10 * hid * wide),
        name="backward_tile",
    )(
        routed,
        one,
        two,
        steep,
        opened,
        weights,
        pulled,
        second,
        head,
        stats,
        near,
        far,
        far_rays,
        far_scaled,
        partial,
        *other_packs,
    )

    mean_error = mean[0] if packed else lax.psum(error[0], ("depth", "lat", "core")) / entries
    return (
        first_grad[None, None],
        second_grad[None, None],
        third_grad[None, None],
        density_grad[None],
        jnp.transpose(decoder_grad, (1, 0, 2)),
        mean_error[0, 0],
    )


def solution(mesh):
    shape = mesh.devices.shape
    split = Mesh(
        mesh.devices.reshape(shape[0], shape[1] // PAIR, PAIR), ("depth", "lat", "core")
    )
    lateral = ("lat", "core")
    placed = (
        P("depth", lateral, None, None),
        P("depth", lateral, None, None),
        P("depth", lateral, None, None),
        P("depth", lateral, None, None),
        P("depth", lateral, None),
        P(lateral, None, None),
        P(lateral, None),
        P(lateral, None),
        P(lateral, None, "depth"),
    )
    return jax.shard_map(
        body,
        mesh=split,
        in_specs=placed,
        out_specs=(
            P("depth", lateral, None, None),
            P("depth", lateral, None, None),
            P("depth", lateral, None, None),
            P("depth", lateral, None),
            P(lateral, None, None),
            P(),
        ),
        check_vma=False,
    )
```

```python
import functools

import jax
import jax.numpy as jnp
from jax import lax
from jax.experimental import pallas as pl
from jax.experimental.pallas import tpu as pltpu
from jax.sharding import Mesh
from jax.sharding import PartitionSpec as P

SAMPLES = 8
SPP = 4
PAIR = 2
STEP = 2
TILE = 8

step_length = 0.04
norm_floor = 1e-05
exact_mode = lax.Precision.HIGHEST

rows_rows = (((1,), (1,)), ((), ()))
lead_lead = (((0,), (0,)), ((), ()))


def dot(left, right, **how):
    return jnp.dot(left, right, preferred_element_type=jnp.float32, **how)


def dot_rows(left, right, **how):
    return lax.dot_general(left, right, rows_rows, preferred_element_type=jnp.float32, **how)


def softplus(value):
    return jnp.maximum(value, 0.0) + jnp.log1p(jnp.exp(-jnp.abs(value)))


def tile_place(order_ref, tile, tile_count):
    place = jnp.int32(0)
    for position in range(tile_count):
        place = place + jnp.where(order_ref[0, position] == tile, position, 0)
    return place


def forward_kernel(
    share,
    slot_rays,
    stride,
    target_of,
    samples_hbm,
    slot_hbm,
    first_hbm,
    second_hbm,
    density_hbm,
    order_hbm,
    third_hbm,
    *rest,
):
    tile_count = order_hbm.shape[1]
    routed_ref, one_ref, two_ref, logit_ref, behind_ref, third_ref = rest[:6]
    sum_refs = rest[6 : 5 + tile_count]
    (
        samples_ref,
        slot_ref,
        first_ref,
        second_ref,
        density_ref,
        order_ref,
        route_ref,
        first_turned,
        second_turned,
        small_sem,
        big_sem,
    ) = rest[5 + tile_count :]
    rays = slot_ref.shape[1]
    enc = samples_ref.shape[0]
    total = samples_ref.shape[1]
    samples = total // rays
    shares = rays // share
    small = [
        pltpu.make_async_copy(far, near, small_sem.at[spot])
        for spot, (far, near) in enumerate(
            (
                (slot_hbm, slot_ref),
                (first_hbm, first_ref),
                (second_hbm, second_ref),
                (density_hbm, density_ref),
                (order_hbm, order_ref),
                (third_hbm, third_ref),
            )
        )
    ]
    parts = 2
    big = []
    for spot in range(parts):
        window = pl.ds(spot * (total // parts), total // parts)
        big.append(
            pltpu.make_async_copy(
                samples_hbm.at[:, window], samples_ref.at[:, window], big_sem.at[spot]
            )
        )
    small[0].start()
    for copy in big:
        copy.start()
    for copy in small[1:]:
        copy.start()
    small[0].wait()
    core = lax.axis_index("core")
    target_row = lax.broadcasted_iota(jnp.int32, (share, share), 0)
    for part in range(shares):
        slots = slot_ref[:, part * share : (part + 1) * share]
        owner = lax.div(slots, jnp.int32(slot_rays))
        inside = slots - owner * slot_rays
        lateral = lax.div(owner, jnp.int32(PAIR))
        side = jnp.bitwise_xor(owner - lateral * PAIR, core)
        place = side * (share // PAIR) + lateral * slot_rays + inside
        route_ref[part] = (target_row == place).astype(jnp.float32).astype(jnp.bfloat16)
    for copy in small[1:5]:
        copy.wait()
    first_turned[...] = first_ref[...].T
    second_turned[...] = second_ref[...].T
    for spot in range(parts):
        big[spot].wait()
        chosen = range(spot * (samples // parts), (spot + 1) * (samples // parts))
        for part in range(shares):
            starts = [sample * rays + part * share for sample in chosen]
            stacked = jnp.concatenate(
                [samples_ref[:, start : start + share] for start in starts], axis=0
            )
            moved = dot_rows(stacked, route_ref[part]).astype(jnp.bfloat16)
            for row, start in enumerate(starts):
                routed_ref[:, start : start + share] = moved[row * enc : (row + 1) * enc]
    passed = jnp.zeros((1, rays), jnp.float32)
    for step in range(total // stride):
        lanes = slice(step * stride, (step + 1) * stride)
        one = jnp.maximum(dot(first_turned[...], routed_ref[:, lanes]), 0.0).astype(jnp.bfloat16)
        one_ref[:, lanes] = one
        two = jnp.maximum(dot(second_turned[...], one), 0.0).astype(jnp.bfloat16)
        two_ref[:, lanes] = two
        logits = dot(density_ref[...], two)
        for part in range(stride // rays):
            sample = step * (stride // rays) + part
            row = logits[:, part * rays : (part + 1) * rays]
            logit_ref[sample : sample + 1] = row
            density = softplus(row)
            passed = passed + density
    depth_sum = step_length * passed
    me = lax.axis_index("depth")
    mine = tile_place(order_ref, me, tile_count)
    for step in range(1, tile_count):
        ahead = mine < tile_place(order_ref, target_of(me, step), tile_count)
        sum_refs[step - 1][...] = jnp.where(ahead, depth_sum, 0.0)
        behind_ref[step - 1 : step] = jnp.where(
            ahead, jnp.zeros((1, 128), jnp.float32), jnp.ones((1, 128), jnp.float32)
        )
    small[5].wait()


def join_kernel(keep_ref, met_ref, joined_ref):
    joined_ref[...] = (
        keep_ref[...].astype(jnp.float32) + met_ref[...].astype(jnp.float32)
    ).astype(jnp.bfloat16)


def gather_kernel(two_ref, logit_ref, gathered_ref):
    samples, rays = logit_ref.shape
    passed = jnp.zeros((1, rays), jnp.float32)
    weights = []
    for sample in range(samples):
        density = softplus(logit_ref[sample : sample + 1])
        weights.append(jnp.exp(-step_length * passed) * (1.0 - jnp.exp(-step_length * density)))
        passed = passed + density
    for start in range(0, rays, 128):
        gathered = None
        for sample in range(samples):
            first = sample * rays + start
            piece = weights[sample][:, start : start + 128] * two_ref[
                :, first : first + 128
            ].astype(jnp.float32)
            gathered = piece if gathered is None else gathered + piece
        gathered_ref[:, start : start + 128] = gathered


def compose(gathered_ref, scale, third_ref, out_ref, side, share):
    half = share // PAIR
    for part in range(gathered_ref.shape[1] // share):
        start = part * share + side * half
        lanes = slice(start, start + half)
        scaled = (gathered_ref[:, lanes] * scale[:, lanes]).T.astype(jnp.bfloat16)
        out_ref[part * half : (part + 1) * half] = dot(scaled, third_ref[...]).astype(jnp.bfloat16)


def send_kernel(share, gathered_ref, *rest):
    others = rest[:-3]
    third_ref, send_ref, scale_ref = rest[-3:]
    before = others[0][...]
    for other in others[1:]:
        before = before + other[...]
    scale = jnp.exp(-before)
    scale_ref[...] = scale
    compose(gathered_ref, scale, third_ref, send_ref, 1, share)


def keep_kernel(share, gathered_ref, scale_ref, third_ref, keep_ref):
    compose(gathered_ref, scale_ref[...], third_ref, keep_ref, 0, share)


def pixel_kernel(
    slot_rays, packed, arrived_ref, decoder_ref, target_ref, back_ref, stat_ref, *square_refs
):
    tile_count, rows, _ = arrived_ref.shape
    members = SPP // PAIR
    groups = rows // slot_rays // members
    pixels = groups * slot_rays
    total = arrived_ref[0].astype(jnp.float32)
    for tile in range(1, tile_count):
        total = total + arrived_ref[tile].astype(jnp.float32)
    pieces = []
    for group in range(groups):
        first = group * members * slot_rays
        piece = total[first : first + slot_rays]
        for member in range(1, members):
            start = first + member * slot_rays
            piece = piece + total[start : start + slot_rays]
        pieces.append(piece)
    pixel_mean = jnp.concatenate(pieces, axis=0) / SPP
    mean_square = jnp.mean(pixel_mean * pixel_mean, axis=1, keepdims=True)
    inverse = lax.rsqrt(mean_square + norm_floor)
    normed = pixel_mean * inverse
    decoder = decoder_ref[:, 0]
    row = lax.broadcasted_iota(jnp.int32, (pixels, pixels), 0)
    lane = lax.broadcasted_iota(jnp.int32, (pixels, pixels), 1)
    group_of = lax.div(row, jnp.int32(slot_rays))
    wanted = (row - group_of * slot_rays) * groups + group_of
    pick = (lane == wanted).astype(jnp.float32)
    target = dot_rows(pick, target_ref[:, 0], precision=exact_mode)
    residue = dot_rows(normed, decoder, precision=exact_mode) - target
    stat_ref[...] = lax.dot_general(
        residue, normed, lead_lead, preferred_element_type=jnp.float32, precision=exact_mode
    )
    square = jnp.sum(jnp.sum(residue * residue, axis=1, keepdims=True), axis=0, keepdims=True)
    for square_ref in square_refs:
        square_ref[...] = jnp.broadcast_to(square, square_ref.shape)
    normed_grad = dot(residue, decoder, precision=exact_mode)
    along = jnp.mean(normed_grad * normed, axis=1, keepdims=True)
    pixel_grad = inverse * (normed_grad - normed * along) / SPP
    spread = []
    for group in range(groups):
        spread += [pixel_grad[group * slot_rays : (group + 1) * slot_rays]] * members
    if not packed:
        block = jnp.concatenate(spread, axis=0).astype(jnp.bfloat16)
        for tile in range(tile_count):
            back_ref[tile] = block
        return
    near = jnp.broadcast_to(square, (1, 128))
    split = []
    for _ in range(3):
        split.append(near.astype(jnp.bfloat16).astype(jnp.float32))
        near = near - split[-1]
    split.append(jnp.zeros((TILE - 3, 128), jnp.float32))
    extra = jnp.concatenate(split, axis=0).astype(jnp.bfloat16)
    height = pixel_grad.shape[1] // 128 * slot_rays + TILE
    for spot, piece in enumerate(spread):
        base = spot * height
        narrow = piece.astype(jnp.bfloat16)
        for tile in range(tile_count):
            for column in range(pixel_grad.shape[1] // 128):
                start = base + column * slot_rays
                back_ref[tile, start : start + slot_rays] = narrow[
                    :, column * 128 : (column + 1) * 128
                ]
            back_ref[tile, base + height - TILE : base + height] = extra


def half_share(ref, part, slot_rays, blocks, feat, packed):
    if not packed:
        half = slot_rays * blocks
        return ref[part * half : (part + 1) * half]
    height = feat // 128 * slot_rays + TILE
    pieces = []
    for block in range(part * blocks, (part + 1) * blocks):
        base = block * height
        pieces.append(
            jnp.concatenate(
                [
                    ref[base + column * slot_rays : base + (column + 1) * slot_rays]
                    for column in range(feat // 128)
                ],
                axis=1,
            )
        )
    return jnp.concatenate(pieces, axis=0)


def pull(third_ref, gathered_ref, scale_ref, ray_grad, side, share):
    rays = gathered_ref.shape[1]
    half = share // PAIR
    starts = range(side * half, rays, share)
    gathered = jnp.concatenate([gathered_ref[:, at : at + half] for at in starts], axis=1)
    scale = jnp.concatenate([scale_ref[:, at : at + half] for at in starts], axis=1)
    scaled = gathered * scale
    pulled = dot_rows(third_ref[...], ray_grad)
    return pulled, scaled, jnp.sum(scaled * pulled, axis=0, keepdims=True)


def near_kernel(
    share,
    rays_of,
    near_ref,
    third_ref,
    gathered_ref,
    scale_ref,
    pulled_ref,
    term_ref,
    partial_ref,
):
    shares = gathered_ref.shape[1] // share
    ray_grad = jnp.concatenate([rays_of(near_ref, part) for part in range(shares)], axis=0)
    pulled, scaled, terms = pull(third_ref, gathered_ref, scale_ref, ray_grad, 0, share)
    pulled_ref[...] = pulled
    term_ref[...] = terms
    partial_ref[...] = dot(scaled.astype(jnp.bfloat16), ray_grad)


def far_kernel(
    share,
    rays_of,
    behind_ref,
    far_ref,
    third_ref,
    gathered_ref,
    scale_ref,
    stat_ref,
    near_pulled_ref,
    near_term_ref,
    pulled_ref,
    term_ref,
    ray_grad_ref,
    scaled_ref,
    *pack_refs,
):
    rays = gathered_ref.shape[1]
    width = stat_ref.shape[1]
    lines = rays // width
    half = share // PAIR
    ray_grad = jnp.concatenate([rays_of(far_ref, part) for part in range(rays // share)], axis=0)
    ray_grad_ref[...] = ray_grad
    pulled, scaled, terms = pull(third_ref, gathered_ref, scale_ref, ray_grad, 1, share)
    scaled_ref[...] = scaled.astype(jnp.bfloat16)
    pieces = []
    for part in range(rays // share):
        lanes = slice(part * share, (part + 1) * share)
        own = slice(part * half, (part + 1) * half)
        pulled_ref[:, lanes] = jnp.concatenate([near_pulled_ref[:, own], pulled[:, own]], axis=1)
        pieces += [near_term_ref[:, own], terms[:, own]]
    terms = jnp.concatenate(pieces, axis=1)
    term_ref[...] = terms
    for step, pack_ref in enumerate(pack_refs):
        for line in range(lines):
            row = terms[:, line * width : (line + 1) * width]
            use = jnp.concatenate([behind_ref[step : step + 1]] * (width // 128), axis=1)
            pack_ref[line : line + 1] = jnp.where(use > 0.0, row, 0.0)
        pack_ref[lines : lines + stat_ref.shape[0]] = stat_ref[...]


def curve_kernel(logit_ref, scale_ref, kept_ref, weight_ref, slope_ref):
    samples, rays = logit_ref.shape
    passed = jnp.zeros((1, rays), jnp.float32)
    for sample in range(samples):
        density = softplus(logit_ref[sample : sample + 1])
        through = jnp.exp(-step_length * passed)
        kept = jnp.exp(-step_length * density)
        kept_ref[sample : sample + 1] = through * kept
        weight_ref[sample : sample + 1] = through * (1.0 - kept) * scale_ref[...]
        passed = passed + density
    slope_ref[...] = step_length * jax.nn.sigmoid(logit_ref[...])


def weight_kernel(
    entries,
    height,
    two_ref,
    scale_ref,
    kept_ref,
    weight_ref,
    pulled_ref,
    term_ref,
    near_ref,
    far_ref,
    far_rays_ref,
    far_scaled_ref,
    partial_ref,
    open_ref,
    third_grad_ref,
    *mean_refs,
):
    third_grad_ref[...] = partial_ref[...] + dot(far_scaled_ref[...], far_rays_ref[...])
    for mean_ref in mean_refs:
        error = None
        for ref in (near_ref, far_ref):
            for base in range(height - TILE, ref.shape[0], height):
                piece = ref[base : base + TILE].astype(jnp.float32)
                error = piece if error is None else error + piece
        mean_ref[...] = jnp.sum(error, axis=0, keepdims=True) / entries
    samples, rays = kept_ref.shape
    scale = scale_ref[...]
    behind = term_ref[...]
    for sample in range(samples):
        pieces = []
        for start in range(0, rays, 256):
            first = sample * rays + start
            two = two_ref[:, first : first + 256].astype(jnp.float32)
            pieces.append(
                jnp.sum(two * pulled_ref[:, start : start + 256], axis=0, keepdims=True)
            )
        weight_grad = jnp.concatenate(pieces, axis=1)
        behind = behind - weight_ref[sample : sample + 1] * weight_grad
        open_ref[sample : sample + 1] = kept_ref[sample : sample + 1] * scale * weight_grad - behind


def backward_kernel(
    share,
    routed_ref,
    one_ref,
    two_ref,
    steep_ref,
    open_ref,
    weight_ref,
    pulled_ref,
    second_ref,
    density_ref,
    stat_ref,
    third_grad_ref,
    *rest,
):
    others = rest[:-12]
    result_hbms = rest[-12:-7]
    back_two_ref, back_one_ref, first_grad_ref, second_grad_ref = rest[-7:-3]
    density_grad_ref, decoder_grad_ref, sem = rest[-3:]
    results = (first_grad_ref, second_grad_ref, third_grad_ref, density_grad_ref, decoder_grad_ref)
    leaving = [
        pltpu.make_async_copy(near, far, sem.at[spot])
        for spot, (near, far) in enumerate(zip(results, result_hbms))
    ]
    leaving[2].start()
    samples, rays = steep_ref.shape
    width = others[0].shape[1]
    lines = rays // width
    colors = stat_ref.shape[0]
    later = others[0][...]
    for other in others[1:]:
        later = later + other[...]
    slope = jnp.concatenate([later[line : line + 1] for line in range(lines)], axis=1)
    for color in range(colors):
        total = later[lines + color : lines + color + 1]
        decoder_grad_ref[color] = total + stat_ref[color : color + 1]
    leaving[4].start()
    logit_grad = ((open_ref[...] - slope) * steep_ref[...]).astype(jnp.bfloat16)
    head = density_ref[...].astype(jnp.float32).T
    hid = one_ref.shape[0]
    strip = min(64, hid)
    first_grad = second_grad = None
    own_grad = [None] * (hid // strip)
    for sample in range(samples):
        lanes = slice(sample * rays, (sample + 1) * rays)
        row = logit_grad[sample : sample + 1].astype(jnp.float32)
        for spot in range(hid // strip):
            rows = slice(spot * strip, (spot + 1) * strip)
            for start in range(0, rays, share):
                part = slice(start, start + share)
                two = two_ref[rows, sample * rays + start : sample * rays + start + share]
                slope_row = row[:, part]
                weighted = (
                    weight_ref[sample : sample + 1, part] * pulled_ref[rows, part]
                    + head[rows] * slope_row
                )
                back_two_ref[rows, part] = jnp.where(
                    two > 0, weighted.astype(jnp.bfloat16), jnp.zeros_like(two)
                )
                product = two.astype(jnp.float32) * slope_row
                for column in range(0, share, 128):
                    piece = product[:, column : column + 128]
                    own_grad[spot] = piece if own_grad[spot] is None else own_grad[spot] + piece
        piece = dot_rows(one_ref[:, lanes], back_two_ref[...])
        second_grad = piece if second_grad is None else second_grad + piece
        if sample == samples - 1:
            second_grad_ref[...] = second_grad
            leaving[1].start()
        for start in range(0, rays, share):
            one = one_ref[:, sample * rays + start : sample * rays + start + share]
            back = dot(second_ref[...], back_two_ref[:, start : start + share])
            back_one_ref[:, start : start + share] = jnp.where(
                one > 0, back.astype(jnp.bfloat16), jnp.zeros_like(one)
            )
        piece = dot_rows(routed_ref[:, lanes], back_one_ref[...])
        first_grad = piece if first_grad is None else first_grad + piece
    first_grad_ref[...] = first_grad
    leaving[0].start()
    density_grad_ref[...] = jnp.sum(
        jnp.concatenate(own_grad, axis=0), axis=1, keepdims=True
    ).T
    leaving[3].start()
    for copy in leaving:
        copy.wait()


def f32(*shape):
    return jax.ShapeDtypeStruct(shape, jnp.float32)


def bf16(*shape):
    return jax.ShapeDtypeStruct(shape, jnp.bfloat16)


def grant(size):
    return pltpu.CompilerParams(vmem_limit_bytes=size * 1024 * 1024)


def cost(flops, moved):
    return pl.CostEstimate(flops=flops, bytes_accessed=moved, transcendentals=0)


def body(samples, w_first, w_second, w_third, w_density, decoder, depth_order, ray_slot, target):
    tile_count = lax.axis_size("depth")
    lateral_count = lax.axis_size("lat")
    column_count = lateral_count * PAIR
    inputs = samples[0, 0]
    first, second, third = w_first[0, 0], w_second[0, 0], w_third[0, 0]
    head = w_density[0]
    enc, hid = first.shape
    feat = third.shape[1]
    ray_total = inputs.shape[1] // SAMPLES
    share = ray_total // tile_count
    slot_rays = share // column_count
    half_rays = ray_total // PAIR
    paired = tile_count & (tile_count - 1) == 0
    wide = SAMPLES * ray_total

    def target_of(me, step):
        if paired:
            return jnp.bitwise_xor(me, step)
        return lax.rem(me + step, tile_count)

    def from_others(values):
        arrived = []
        for step in reversed(range(1, tile_count)):
            moves = [
                (tile, tile ^ step if paired else (tile + step) % tile_count)
                for tile in range(tile_count)
            ]
            arrived.append(lax.ppermute(values[step - 1], "depth", moves))
        return arrived

    swap = [(0, 1), (1, 0)]
    vmem = pl.BlockSpec(memory_space=pltpu.VMEM)
    anywhere = pl.BlockSpec(memory_space=pl.ANY)
    stride = ray_total * STEP

    routed, one, two, logits, behind, third_near, *sums = pl.pallas_call(
        functools.partial(forward_kernel, share, slot_rays, stride, target_of),
        out_shape=(
            pltpu.VMEM((enc, wide), jnp.bfloat16),
            pltpu.VMEM((hid, wide), jnp.bfloat16),
            pltpu.VMEM((hid, wide), jnp.bfloat16),
            f32(SAMPLES, ray_total),
            f32(tile_count - 1, 128),
            pltpu.VMEM((hid, feat), jnp.bfloat16),
        )
        + (f32(1, ray_total),) * (tile_count - 1),
        in_specs=[anywhere] * 7,
        out_specs=(vmem,) * (tile_count + 5),
        scratch_shapes=[
            pltpu.VMEM((enc, wide), jnp.bfloat16),
            pltpu.VMEM((1, ray_total), jnp.int32),
            pltpu.VMEM((enc, hid), jnp.bfloat16),
            pltpu.VMEM((hid, hid), jnp.bfloat16),
            pltpu.VMEM((1, hid), jnp.bfloat16),
            pltpu.SMEM((1, tile_count), jnp.int32),
            pltpu.VMEM((tile_count, share, share), jnp.bfloat16),
            pltpu.VMEM((hid, enc), jnp.bfloat16),
            pltpu.VMEM((hid, hid), jnp.bfloat16),
            pltpu.SemaphoreType.DMA((6,)),
            pltpu.SemaphoreType.DMA((2,)),
        ],
        compiler_params=grant(32),
        name="forward_tile",
    )(
        *[
            pltpu.with_memory_space_constraint(value, pltpu.HBM)
            for value in (inputs, ray_slot, first, second, head, depth_order, third)
        ]
    )

    other_sums = from_others(sums)
    routed, one, two, third_near = (
        pltpu.with_memory_space_constraint(value, pltpu.VMEM)
        for value in (routed, one, two, third_near)
    )
    gathered = pl.pallas_call(
        gather_kernel,
        out_shape=f32(hid, ray_total),
        in_specs=[vmem] * 2,
        out_specs=vmem,
        compiler_params=grant(16),
        cost_estimate=cost(4 * hid * wide, 3 * hid * wide),
        name="gather_samples",
    )(two, logits)
    send, scale = pl.pallas_call(
        functools.partial(send_kernel, share),
        out_shape=(bf16(half_rays, feat), f32(1, ray_total)),
        in_specs=[vmem] * (tile_count + 1),
        out_specs=(vmem,) * 2,
        compiler_params=grant(16),
        cost_estimate=cost(0, 20 * feat * half_rays),
        name="send_rays",
    )(gathered, *other_sums, third_near)
    keep = pl.pallas_call(
        functools.partial(keep_kernel, share),
        out_shape=bf16(half_rays, feat),
        in_specs=[vmem] * 3,
        out_specs=vmem,
        compiler_params=grant(16),
        cost_estimate=cost(0, 20 * feat * half_rays),
        name="keep_rays",
    )(gathered, scale, third_near)

    met = lax.ppermute(send, "core", swap)
    joined = pl.pallas_call(
        join_kernel,
        out_shape=bf16(half_rays, feat),
        in_specs=[vmem] * 2,
        out_specs=vmem,
        compiler_params=grant(16),
        name="join_pair",
    )(keep, met)
    arrived = lax.all_to_all(
        joined.reshape(tile_count * lateral_count, slot_rays, feat),
        ("depth", "lat"),
        split_axis=0,
        concat_axis=0,
        tiled=True,
    )
    packed = slot_rays % 16 == 0
    height = feat // 128 * slot_rays + TILE if packed else slot_rays
    width = 128 if packed else feat
    rays_of = functools.partial(
        half_share, slot_rays=slot_rays, blocks=lateral_count, feat=feat, packed=packed
    )
    entries = decoder.shape[1] * column_count * (ray_total // SPP)
    decoder_lines = jnp.transpose(decoder, (1, 0, 2))
    target_lines = jnp.transpose(target, (1, 0, 2))
    back, stats, *error = pl.pallas_call(
        functools.partial(pixel_kernel, slot_rays, packed),
        out_shape=(
            bf16(tile_count, lateral_count * height, width),
            f32(decoder.shape[1], feat),
        )
        + (f32(1, 128),) * int(not packed),
        in_specs=[vmem] * 3,
        out_specs=(vmem,) * (2 + int(not packed)),
        compiler_params=grant(16),
        cost_estimate=cost(0, 200 * feat * half_rays),
        name="pixel_loss",
    )(arrived.reshape(tile_count, lateral_count * slot_rays, feat), decoder_lines, target_lines)

    near = lax.all_to_all(
        back.reshape(tile_count * lateral_count, height, width),
        ("depth", "lat"),
        split_axis=0,
        concat_axis=0,
        tiled=True,
    ).reshape(tile_count * lateral_count * height, width)
    far = lax.ppermute(near, "core", swap)

    kept, weights, steep = pl.pallas_call(
        curve_kernel,
        out_shape=(f32(SAMPLES, ray_total),) * 3,
        in_specs=[vmem] * 2,
        out_specs=(vmem,) * 3,
        compiler_params=grant(16),
        cost_estimate=cost(0, 16 * hid * ray_total),
        name="ray_curves",
    )(logits, scale)

    lines = ray_total // feat
    pack_rows = lines + decoder.shape[1]
    pack_rows = lines + decoder.shape[1]
    near_pulled, near_terms, partial = pl.pallas_call(
        functools.partial(near_kernel, share, rays_of),
        out_shape=(f32(hid, half_rays), f32(1, half_rays), f32(hid, feat)),
        in_specs=[vmem] * 4,
        out_specs=(vmem,) * 3,
        compiler_params=grant(16),
        cost_estimate=cost(4 * hid * feat * half_rays, 8 * hid * ray_total),
        name="near_rays",
    )(near, third_near, gathered, scale)
    pulled, terms, far_rays, far_scaled, *packs = pl.pallas_call(
        functools.partial(far_kernel, share, rays_of),
        out_shape=(f32(hid, ray_total), f32(1, ray_total), bf16(half_rays, feat), bf16(hid, half_rays))
        + (f32(pack_rows, feat),) * (tile_count - 1),
        in_specs=[vmem] * 8,
        out_specs=(vmem,) * (3 + tile_count),
        compiler_params=grant(16),
        cost_estimate=cost(0, 50 * feat * half_rays),
        name="far_rays",
    )(behind, far, third_near, gathered, scale, stats, near_pulled, near_terms)

    other_packs = from_others(packs)
    opened, third_near_grad, *mean = pl.pallas_call(
        functools.partial(weight_kernel, entries, height),
        out_shape=(f32(SAMPLES, ray_total), pltpu.VMEM((hid, feat), jnp.float32))
        + (f32(1, 128),) * int(packed),
        in_specs=[vmem] * 11,
        out_specs=(vmem,) * (2 + int(packed)),
        compiler_params=grant(16),
        cost_estimate=cost(0, 3 * hid * wide),
        name="weight_gradient",
    )(two, scale, kept, weights, pulled, terms, near, far, far_rays, far_scaled, partial)
    third_near_grad = pltpu.with_memory_space_constraint(third_near_grad, pltpu.VMEM)
    results = [(enc, hid), (hid, hid), (hid, feat), (1, hid), (decoder.shape[1], 1, feat)]
    first_grad, second_grad, third_grad, density_grad, decoder_grad = pl.pallas_call(
        functools.partial(backward_kernel, share),
        out_shape=tuple(f32(*shape) for shape in results),
        in_specs=[vmem] * (10 + tile_count),
        out_specs=(anywhere,) * len(results),
        scratch_shapes=[pltpu.VMEM((hid, ray_total), jnp.bfloat16)] * 2
        + [pltpu.VMEM(shape, jnp.float32) for shape in results[:2] + results[3:]]
        + [pltpu.SemaphoreType.DMA((len(results),))],
        compiler_params=grant(20),
        cost_estimate=cost(6 * hid * hid * wide, 10 * hid * wide),
        name="backward_tile",
    )(
        routed,
        one,
        two,
        steep,
        opened,
        weights,
        pulled,
        second,
        head,
        stats,
        third_near_grad,
        *other_packs,
    )

    mean_error = mean[0] if packed else lax.psum(error[0], ("depth", "lat", "core")) / entries
    return (
        first_grad[None, None],
        second_grad[None, None],
        third_grad[None, None],
        density_grad[None],
        jnp.transpose(decoder_grad, (1, 0, 2)),
        mean_error[0, 0],
    )


def solution(mesh):
    shape = mesh.devices.shape
    split = Mesh(
        mesh.devices.reshape(shape[0], shape[1] // PAIR, PAIR), ("depth", "lat", "core")
    )
    lateral = ("lat", "core")
    placed = (
        P("depth", lateral, None, None),
        P("depth", lateral, None, None),
        P("depth", lateral, None, None),
        P("depth", lateral, None, None),
        P("depth", lateral, None),
        P(lateral, None, None),
        P(lateral, None),
        P(lateral, None),
        P(lateral, None, "depth"),
    )
    return jax.shard_map(
        body,
        mesh=split,
        in_specs=placed,
        out_specs=(
            P("depth", lateral, None, None),
            P("depth", lateral, None, None),
            P("depth", lateral, None, None),
            P("depth", lateral, None),
            P(lateral, None, None),
            P(),
        ),
        check_vma=False,
    )
```

```python
import functools

import jax
import jax.numpy as jnp
from jax import lax
from jax.experimental import pallas as pl
from jax.experimental.pallas import tpu as pltpu
from jax.sharding import Mesh
from jax.sharding import PartitionSpec as P

SAMPLES = 8
SPP = 4
PAIR = 2
STEP = 2
TILE = 16

step_length = 0.04
norm_floor = 1e-05
exact_mode = lax.Precision.HIGHEST

rows_rows = (((1,), (1,)), ((), ()))
lead_lead = (((0,), (0,)), ((), ()))


def dot(left, right, **how):
    return jnp.dot(left, right, preferred_element_type=jnp.float32, **how)


def dot_rows(left, right, **how):
    return lax.dot_general(left, right, rows_rows, preferred_element_type=jnp.float32, **how)


def softplus(value):
    return jnp.maximum(value, 0.0) + jnp.log1p(jnp.exp(-jnp.abs(value)))


def tile_place(order_ref, tile, tile_count):
    place = jnp.int32(0)
    for position in range(tile_count):
        place = place + jnp.where(order_ref[0, position] == tile, position, 0)
    return place


def forward_kernel(
    share,
    slot_rays,
    stride,
    target_of,
    samples_hbm,
    slot_hbm,
    first_hbm,
    second_hbm,
    density_hbm,
    order_hbm,
    third_hbm,
    *rest,
):
    tile_count = order_hbm.shape[1]
    routed_ref, one_ref, two_ref, logit_ref, behind_ref, third_ref = rest[:6]
    sum_refs = rest[6 : 5 + tile_count]
    (
        samples_ref,
        slot_ref,
        first_ref,
        second_ref,
        density_ref,
        order_ref,
        route_ref,
        first_turned,
        second_turned,
        small_sem,
        big_sem,
    ) = rest[5 + tile_count :]
    rays = slot_ref.shape[1]
    enc = samples_ref.shape[0]
    total = samples_ref.shape[1]
    samples = total // rays
    shares = rays // share
    small = [
        pltpu.make_async_copy(far, near, small_sem.at[spot])
        for spot, (far, near) in enumerate(
            (
                (slot_hbm, slot_ref),
                (first_hbm, first_ref),
                (second_hbm, second_ref),
                (density_hbm, density_ref),
                (order_hbm, order_ref),
                (third_hbm, third_ref),
            )
        )
    ]
    parts = 2
    big = []
    for spot in range(parts):
        window = pl.ds(spot * (total // parts), total // parts)
        big.append(
            pltpu.make_async_copy(
                samples_hbm.at[:, window], samples_ref.at[:, window], big_sem.at[spot]
            )
        )
    small[0].start()
    for copy in big:
        copy.start()
    for copy in small[1:]:
        copy.start()
    small[0].wait()
    core = lax.axis_index("core")
    target_row = lax.broadcasted_iota(jnp.int32, (share, share), 0)
    for part in range(shares):
        slots = slot_ref[:, part * share : (part + 1) * share]
        owner = lax.div(slots, jnp.int32(slot_rays))
        inside = slots - owner * slot_rays
        lateral = lax.div(owner, jnp.int32(PAIR))
        side = jnp.bitwise_xor(owner - lateral * PAIR, core)
        place = side * (share // PAIR) + lateral * slot_rays + inside
        route_ref[part] = (target_row == place).astype(jnp.float32).astype(jnp.bfloat16)
    for copy in small[1:5]:
        copy.wait()
    first_turned[...] = first_ref[...].T
    second_turned[...] = second_ref[...].T
    for spot in range(parts):
        big[spot].wait()
        chosen = range(spot * (samples // parts), (spot + 1) * (samples // parts))
        for part in range(shares):
            starts = [sample * rays + part * share for sample in chosen]
            stacked = jnp.concatenate(
                [samples_ref[:, start : start + share] for start in starts], axis=0
            )
            moved = dot_rows(stacked, route_ref[part]).astype(jnp.bfloat16)
            for row, start in enumerate(starts):
                routed_ref[:, start : start + share] = moved[row * enc : (row + 1) * enc]
    passed = jnp.zeros((1, rays), jnp.float32)
    for step in range(total // stride):
        lanes = slice(step * stride, (step + 1) * stride)
        one = jnp.maximum(dot(first_turned[...], routed_ref[:, lanes]), 0.0).astype(jnp.bfloat16)
        one_ref[:, lanes] = one
        two = jnp.maximum(dot(second_turned[...], one), 0.0).astype(jnp.bfloat16)
        two_ref[:, lanes] = two
        logits = dot(density_ref[...], two)
        for part in range(stride // rays):
            sample = step * (stride // rays) + part
            row = logits[:, part * rays : (part + 1) * rays]
            logit_ref[sample : sample + 1] = row
            density = softplus(row)
            passed = passed + density
    depth_sum = step_length * passed
    me = lax.axis_index("depth")
    mine = tile_place(order_ref, me, tile_count)
    for step in range(1, tile_count):
        ahead = mine < tile_place(order_ref, target_of(me, step), tile_count)
        sum_refs[step - 1][...] = jnp.where(ahead, depth_sum, 0.0)
        behind_ref[step - 1 : step] = jnp.where(
            ahead, jnp.zeros((1, 128), jnp.float32), jnp.ones((1, 128), jnp.float32)
        )
    small[5].wait()


def join_kernel(keep_ref, met_ref, joined_ref):
    joined_ref[...] = (
        keep_ref[...].astype(jnp.float32) + met_ref[...].astype(jnp.float32)
    ).astype(jnp.bfloat16)


def gather_kernel(two_ref, logit_ref, gathered_ref):
    samples, rays = logit_ref.shape
    passed = jnp.zeros((1, rays), jnp.float32)
    weights = []
    for sample in range(samples):
        density = softplus(logit_ref[sample : sample + 1])
        weights.append(jnp.exp(-step_length * passed) * (1.0 - jnp.exp(-step_length * density)))
        passed = passed + density
    for start in range(0, rays, 128):
        gathered = None
        for sample in range(samples):
            first = sample * rays + start
            piece = weights[sample][:, start : start + 128] * two_ref[
                :, first : first + 128
            ].astype(jnp.float32)
            gathered = piece if gathered is None else gathered + piece
        gathered_ref[:, start : start + 128] = gathered


def compose(gathered_ref, scale, third_ref, out_ref, side, share):
    half = share // PAIR
    for part in range(gathered_ref.shape[1] // share):
        start = part * share + side * half
        lanes = slice(start, start + half)
        scaled = (gathered_ref[:, lanes] * scale[:, lanes]).T.astype(jnp.bfloat16)
        out_ref[part * half : (part + 1) * half] = dot(scaled, third_ref[...]).astype(jnp.bfloat16)


def send_kernel(share, gathered_ref, *rest):
    others = rest[:-3]
    third_ref, send_ref, scale_ref = rest[-3:]
    before = others[0][...]
    for other in others[1:]:
        before = before + other[...]
    scale = jnp.exp(-before)
    scale_ref[...] = scale
    compose(gathered_ref, scale, third_ref, send_ref, 1, share)


def keep_kernel(share, gathered_ref, scale_ref, third_ref, keep_ref):
    compose(gathered_ref, scale_ref[...], third_ref, keep_ref, 0, share)


def pixel_kernel(
    slot_rays, packed, arrived_ref, decoder_ref, target_ref, back_ref, stat_ref, *square_refs
):
    tile_count, rows, _ = arrived_ref.shape
    members = SPP // PAIR
    groups = rows // slot_rays // members
    pixels = groups * slot_rays
    total = arrived_ref[0].astype(jnp.float32)
    for tile in range(1, tile_count):
        total = total + arrived_ref[tile].astype(jnp.float32)
    pieces = []
    for group in range(groups):
        first = group * members * slot_rays
        piece = total[first : first + slot_rays]
        for member in range(1, members):
            start = first + member * slot_rays
            piece = piece + total[start : start + slot_rays]
        pieces.append(piece)
    pixel_mean = jnp.concatenate(pieces, axis=0) / SPP
    mean_square = jnp.mean(pixel_mean * pixel_mean, axis=1, keepdims=True)
    inverse = lax.rsqrt(mean_square + norm_floor)
    normed = pixel_mean * inverse
    decoder = decoder_ref[:, 0]
    row = lax.broadcasted_iota(jnp.int32, (pixels, pixels), 0)
    lane = lax.broadcasted_iota(jnp.int32, (pixels, pixels), 1)
    group_of = lax.div(row, jnp.int32(slot_rays))
    wanted = (row - group_of * slot_rays) * groups + group_of
    pick = (lane == wanted).astype(jnp.float32)
    target = dot_rows(pick, target_ref[:, 0], precision=exact_mode)
    residue = dot_rows(normed, decoder, precision=exact_mode) - target
    stat_ref[...] = lax.dot_general(
        residue, normed, lead_lead, preferred_element_type=jnp.float32, precision=exact_mode
    )
    square = jnp.sum(jnp.sum(residue * residue, axis=1, keepdims=True), axis=0, keepdims=True)
    for square_ref in square_refs:
        square_ref[...] = jnp.broadcast_to(square, square_ref.shape)
    normed_grad = dot(residue, decoder, precision=exact_mode)
    along = jnp.mean(normed_grad * normed, axis=1, keepdims=True)
    pixel_grad = inverse * (normed_grad - normed * along) / SPP
    spread = []
    for group in range(groups):
        spread += [pixel_grad[group * slot_rays : (group + 1) * slot_rays]] * members
    if not packed:
        block = jnp.concatenate(spread, axis=0).astype(jnp.bfloat16)
        for tile in range(tile_count):
            back_ref[tile] = block
        return
    near = jnp.broadcast_to(square, (1, 128))
    split = []
    for _ in range(3):
        split.append(near.astype(jnp.bfloat16).astype(jnp.float32))
        near = near - split[-1]
    split.append(jnp.zeros((TILE - 3, 128), jnp.float32))
    extra = jnp.concatenate(split, axis=0).astype(jnp.bfloat16)
    height = pixel_grad.shape[1] // 128 * slot_rays + TILE
    for spot, piece in enumerate(spread):
        base = spot * height
        narrow = piece.astype(jnp.bfloat16)
        for tile in range(tile_count):
            for column in range(pixel_grad.shape[1] // 128):
                start = base + column * slot_rays
                back_ref[tile, start : start + slot_rays] = narrow[
                    :, column * 128 : (column + 1) * 128
                ]
            back_ref[tile, base + height - TILE : base + height] = extra


def half_share(ref, part, slot_rays, blocks, feat, packed):
    if not packed:
        half = slot_rays * blocks
        return ref[part * half : (part + 1) * half]
    height = feat // 128 * slot_rays + TILE
    pieces = []
    for block in range(part * blocks, (part + 1) * blocks):
        base = block * height
        pieces.append(
            jnp.concatenate(
                [
                    ref[base + column * slot_rays : base + (column + 1) * slot_rays]
                    for column in range(feat // 128)
                ],
                axis=1,
            )
        )
    return jnp.concatenate(pieces, axis=0)


def pull(third_ref, gathered_ref, scale_ref, ray_grad, side, share):
    rays = gathered_ref.shape[1]
    half = share // PAIR
    starts = range(side * half, rays, share)
    gathered = jnp.concatenate([gathered_ref[:, at : at + half] for at in starts], axis=1)
    scale = jnp.concatenate([scale_ref[:, at : at + half] for at in starts], axis=1)
    scaled = gathered * scale
    pulled = dot_rows(third_ref[...], ray_grad)
    return pulled, scaled, jnp.sum(scaled * pulled, axis=0, keepdims=True)


def near_kernel(
    share,
    rays_of,
    near_ref,
    third_ref,
    gathered_ref,
    scale_ref,
    pulled_ref,
    term_ref,
    partial_ref,
):
    shares = gathered_ref.shape[1] // share
    ray_grad = jnp.concatenate([rays_of(near_ref, part) for part in range(shares)], axis=0)
    pulled, scaled, terms = pull(third_ref, gathered_ref, scale_ref, ray_grad, 0, share)
    pulled_ref[...] = pulled
    term_ref[...] = terms
    partial_ref[...] = dot(scaled.astype(jnp.bfloat16), ray_grad)


def far_kernel(
    share,
    rays_of,
    behind_ref,
    far_ref,
    third_ref,
    gathered_ref,
    scale_ref,
    stat_ref,
    near_pulled_ref,
    near_term_ref,
    pulled_ref,
    term_ref,
    ray_grad_ref,
    scaled_ref,
    *pack_refs,
):
    rays = gathered_ref.shape[1]
    width = stat_ref.shape[1]
    lines = rays // width
    half = share // PAIR
    ray_grad = jnp.concatenate([rays_of(far_ref, part) for part in range(rays // share)], axis=0)
    ray_grad_ref[...] = ray_grad
    pulled, scaled, terms = pull(third_ref, gathered_ref, scale_ref, ray_grad, 1, share)
    scaled_ref[...] = scaled.astype(jnp.bfloat16)
    pieces = []
    for part in range(rays // share):
        lanes = slice(part * share, (part + 1) * share)
        own = slice(part * half, (part + 1) * half)
        pulled_ref[:, lanes] = jnp.concatenate([near_pulled_ref[:, own], pulled[:, own]], axis=1)
        pieces += [near_term_ref[:, own], terms[:, own]]
    terms = jnp.concatenate(pieces, axis=1)
    term_ref[...] = terms
    for step, pack_ref in enumerate(pack_refs):
        for line in range(lines):
            row = terms[:, line * width : (line + 1) * width]
            use = jnp.concatenate([behind_ref[step : step + 1]] * (width // 128), axis=1)
            pack_ref[line : line + 1] = jnp.where(use > 0.0, row, 0.0)
        pack_ref[lines : lines + stat_ref.shape[0]] = stat_ref[...]


def curve_kernel(logit_ref, scale_ref, kept_ref, weight_ref, slope_ref):
    samples, rays = logit_ref.shape
    passed = jnp.zeros((1, rays), jnp.float32)
    for sample in range(samples):
        density = softplus(logit_ref[sample : sample + 1])
        through = jnp.exp(-step_length * passed)
        kept = jnp.exp(-step_length * density)
        kept_ref[sample : sample + 1] = through * kept
        weight_ref[sample : sample + 1] = through * (1.0 - kept) * scale_ref[...]
        passed = passed + density
    slope_ref[...] = step_length * jax.nn.sigmoid(logit_ref[...])


def weight_kernel(
    entries,
    height,
    two_ref,
    scale_ref,
    kept_ref,
    weight_ref,
    pulled_ref,
    term_ref,
    near_ref,
    far_ref,
    far_rays_ref,
    far_scaled_ref,
    partial_ref,
    open_ref,
    third_grad_ref,
    *mean_refs,
):
    third_grad_ref[...] = partial_ref[...] + dot(far_scaled_ref[...], far_rays_ref[...])
    for mean_ref in mean_refs:
        error = None
        for ref in (near_ref, far_ref):
            for base in range(height - TILE, ref.shape[0], height):
                piece = ref[base : base + TILE].astype(jnp.float32)
                error = piece if error is None else error + piece
        mean_ref[...] = jnp.sum(error, axis=0, keepdims=True) / entries
    samples, rays = kept_ref.shape
    scale = scale_ref[...]
    behind = term_ref[...]
    for sample in range(samples):
        pieces = []
        for start in range(0, rays, 256):
            first = sample * rays + start
            two = two_ref[:, first : first + 256].astype(jnp.float32)
            pieces.append(
                jnp.sum(two * pulled_ref[:, start : start + 256], axis=0, keepdims=True)
            )
        weight_grad = jnp.concatenate(pieces, axis=1)
        behind = behind - weight_ref[sample : sample + 1] * weight_grad
        open_ref[sample : sample + 1] = kept_ref[sample : sample + 1] * scale * weight_grad - behind


def backward_kernel(
    share,
    routed_ref,
    one_ref,
    two_ref,
    steep_ref,
    open_ref,
    weight_ref,
    pulled_ref,
    second_ref,
    density_ref,
    stat_ref,
    third_grad_ref,
    *rest,
):
    others = rest[:-12]
    result_hbms = rest[-12:-7]
    back_two_ref, back_one_ref, first_grad_ref, second_grad_ref = rest[-7:-3]
    density_grad_ref, decoder_grad_ref, sem = rest[-3:]
    results = (first_grad_ref, second_grad_ref, third_grad_ref, density_grad_ref, decoder_grad_ref)
    leaving = [
        pltpu.make_async_copy(near, far, sem.at[spot])
        for spot, (near, far) in enumerate(zip(results, result_hbms))
    ]
    leaving[2].start()
    samples, rays = steep_ref.shape
    width = others[0].shape[1]
    lines = rays // width
    colors = stat_ref.shape[0]
    later = others[0][...]
    for other in others[1:]:
        later = later + other[...]
    slope = jnp.concatenate([later[line : line + 1] for line in range(lines)], axis=1)
    for color in range(colors):
        total = later[lines + color : lines + color + 1]
        decoder_grad_ref[color] = total + stat_ref[color : color + 1]
    leaving[4].start()
    logit_grad = ((open_ref[...] - slope) * steep_ref[...]).astype(jnp.bfloat16)
    head = density_ref[...].astype(jnp.float32).T
    hid = one_ref.shape[0]
    strip = min(64, hid)
    first_grad = second_grad = None
    own_grad = [None] * (hid // strip)
    for sample in range(samples):
        lanes = slice(sample * rays, (sample + 1) * rays)
        row = logit_grad[sample : sample + 1].astype(jnp.float32)
        for spot in range(hid // strip):
            rows = slice(spot * strip, (spot + 1) * strip)
            for start in range(0, rays, share):
                part = slice(start, start + share)
                two = two_ref[rows, sample * rays + start : sample * rays + start + share]
                slope_row = row[:, part]
                weighted = (
                    weight_ref[sample : sample + 1, part] * pulled_ref[rows, part]
                    + head[rows] * slope_row
                )
                back_two_ref[rows, part] = jnp.where(
                    two > 0, weighted.astype(jnp.bfloat16), jnp.zeros_like(two)
                )
                product = two.astype(jnp.float32) * slope_row
                for column in range(0, share, 128):
                    piece = product[:, column : column + 128]
                    own_grad[spot] = piece if own_grad[spot] is None else own_grad[spot] + piece
        piece = dot_rows(one_ref[:, lanes], back_two_ref[...])
        second_grad = piece if second_grad is None else second_grad + piece
        if sample == samples - 1:
            second_grad_ref[...] = second_grad
            leaving[1].start()
        for start in range(0, rays, share):
            one = one_ref[:, sample * rays + start : sample * rays + start + share]
            back = dot(second_ref[...], back_two_ref[:, start : start + share])
            back_one_ref[:, start : start + share] = jnp.where(
                one > 0, back.astype(jnp.bfloat16), jnp.zeros_like(one)
            )
        piece = dot_rows(routed_ref[:, lanes], back_one_ref[...])
        first_grad = piece if first_grad is None else first_grad + piece
    first_grad_ref[...] = first_grad
    leaving[0].start()
    density_grad_ref[...] = jnp.sum(
        jnp.concatenate(own_grad, axis=0), axis=1, keepdims=True
    ).T
    leaving[3].start()
    for copy in leaving:
        copy.wait()


def f32(*shape):
    return jax.ShapeDtypeStruct(shape, jnp.float32)


def bf16(*shape):
    return jax.ShapeDtypeStruct(shape, jnp.bfloat16)


def grant(size):
    return pltpu.CompilerParams(vmem_limit_bytes=size * 1024 * 1024)


def cost(flops, moved):
    return pl.CostEstimate(flops=flops, bytes_accessed=moved, transcendentals=0)


def body(samples, w_first, w_second, w_third, w_density, decoder, depth_order, ray_slot, target):
    tile_count = lax.axis_size("depth")
    lateral_count = lax.axis_size("lat")
    column_count = lateral_count * PAIR
    inputs = samples[0, 0]
    first, second, third = w_first[0, 0], w_second[0, 0], w_third[0, 0]
    head = w_density[0]
    enc, hid = first.shape
    feat = third.shape[1]
    ray_total = inputs.shape[1] // SAMPLES
    share = ray_total // tile_count
    slot_rays = share // column_count
    half_rays = ray_total // PAIR
    paired = tile_count & (tile_count - 1) == 0
    wide = SAMPLES * ray_total

    def target_of(me, step):
        if paired:
            return jnp.bitwise_xor(me, step)
        return lax.rem(me + step, tile_count)

    def from_others(values):
        arrived = []
        for step in reversed(range(1, tile_count)):
            moves = [
                (tile, tile ^ step if paired else (tile + step) % tile_count)
                for tile in range(tile_count)
            ]
            arrived.append(lax.ppermute(values[step - 1], "depth", moves))
        return arrived

    swap = [(0, 1), (1, 0)]
    vmem = pl.BlockSpec(memory_space=pltpu.VMEM)
    anywhere = pl.BlockSpec(memory_space=pl.ANY)
    stride = ray_total * STEP

    routed, one, two, logits, behind, third_near, *sums = pl.pallas_call(
        functools.partial(forward_kernel, share, slot_rays, stride, target_of),
        out_shape=(
            pltpu.VMEM((enc, wide), jnp.bfloat16),
            pltpu.VMEM((hid, wide), jnp.bfloat16),
            pltpu.VMEM((hid, wide), jnp.bfloat16),
            f32(SAMPLES, ray_total),
            f32(tile_count - 1, 128),
            pltpu.VMEM((hid, feat), jnp.bfloat16),
        )
        + (f32(1, ray_total),) * (tile_count - 1),
        in_specs=[anywhere] * 7,
        out_specs=(vmem,) * (tile_count + 5),
        scratch_shapes=[
            pltpu.VMEM((enc, wide), jnp.bfloat16),
            pltpu.VMEM((1, ray_total), jnp.int32),
            pltpu.VMEM((enc, hid), jnp.bfloat16),
            pltpu.VMEM((hid, hid), jnp.bfloat16),
            pltpu.VMEM((1, hid), jnp.bfloat16),
            pltpu.SMEM((1, tile_count), jnp.int32),
            pltpu.VMEM((tile_count, share, share), jnp.bfloat16),
            pltpu.VMEM((hid, enc), jnp.bfloat16),
            pltpu.VMEM((hid, hid), jnp.bfloat16),
            pltpu.SemaphoreType.DMA((6,)),
            pltpu.SemaphoreType.DMA((2,)),
        ],
        compiler_params=grant(32),
        name="forward_tile",
    )(
        *[
            pltpu.with_memory_space_constraint(value, pltpu.HBM)
            for value in (inputs, ray_slot, first, second, head, depth_order, third)
        ]
    )

    other_sums = from_others(sums)
    routed, one, two, third_near = (
        pltpu.with_memory_space_constraint(value, pltpu.VMEM)
        for value in (routed, one, two, third_near)
    )
    gathered = pl.pallas_call(
        gather_kernel,
        out_shape=f32(hid, ray_total),
        in_specs=[vmem] * 2,
        out_specs=vmem,
        compiler_params=grant(16),
        cost_estimate=cost(4 * hid * wide, 3 * hid * wide),
        name="gather_samples",
    )(two, logits)
    send, scale = pl.pallas_call(
        functools.partial(send_kernel, share),
        out_shape=(bf16(half_rays, feat), f32(1, ray_total)),
        in_specs=[vmem] * (tile_count + 1),
        out_specs=(vmem,) * 2,
        compiler_params=grant(16),
        cost_estimate=cost(0, 20 * feat * half_rays),
        name="send_rays",
    )(gathered, *other_sums, third_near)
    keep = pl.pallas_call(
        functools.partial(keep_kernel, share),
        out_shape=bf16(half_rays, feat),
        in_specs=[vmem] * 3,
        out_specs=vmem,
        compiler_params=grant(16),
        cost_estimate=cost(0, 20 * feat * half_rays),
        name="keep_rays",
    )(gathered, scale, third_near)

    met = lax.ppermute(send, "core", swap)
    joined = pl.pallas_call(
        join_kernel,
        out_shape=bf16(half_rays, feat),
        in_specs=[vmem] * 2,
        out_specs=vmem,
        compiler_params=grant(16),
        name="join_pair",
    )(keep, met)
    arrived = lax.all_to_all(
        joined.reshape(tile_count * lateral_count, slot_rays, feat),
        ("depth", "lat"),
        split_axis=0,
        concat_axis=0,
        tiled=True,
    )
    packed = slot_rays % 16 == 0
    height = feat // 128 * slot_rays + TILE if packed else slot_rays
    width = 128 if packed else feat
    rays_of = functools.partial(
        half_share, slot_rays=slot_rays, blocks=lateral_count, feat=feat, packed=packed
    )
    entries = decoder.shape[1] * column_count * (ray_total // SPP)
    decoder_lines = jnp.transpose(decoder, (1, 0, 2))
    target_lines = jnp.transpose(target, (1, 0, 2))
    back, stats, *error = pl.pallas_call(
        functools.partial(pixel_kernel, slot_rays, packed),
        out_shape=(
            bf16(tile_count, lateral_count * height, width),
            f32(decoder.shape[1], feat),
        )
        + (f32(1, 128),) * int(not packed),
        in_specs=[vmem] * 3,
        out_specs=(vmem,) * (2 + int(not packed)),
        compiler_params=grant(16),
        cost_estimate=cost(0, 200 * feat * half_rays),
        name="pixel_loss",
    )(arrived.reshape(tile_count, lateral_count * slot_rays, feat), decoder_lines, target_lines)

    near = lax.all_to_all(
        back.reshape(tile_count * lateral_count, height, width),
        ("depth", "lat"),
        split_axis=0,
        concat_axis=0,
        tiled=True,
    ).reshape(tile_count * lateral_count * height, width)
    far = lax.ppermute(near, "core", swap)

    kept, weights, steep = pl.pallas_call(
        curve_kernel,
        out_shape=(f32(SAMPLES, ray_total),) * 3,
        in_specs=[vmem] * 2,
        out_specs=(vmem,) * 3,
        compiler_params=grant(16),
        cost_estimate=cost(0, 16 * hid * ray_total),
        name="ray_curves",
    )(logits, scale)

    lines = ray_total // feat
    pack_rows = lines + decoder.shape[1]
    pack_rows = lines + decoder.shape[1]
    near_pulled, near_terms, partial = pl.pallas_call(
        functools.partial(near_kernel, share, rays_of),
        out_shape=(f32(hid, half_rays), f32(1, half_rays), f32(hid, feat)),
        in_specs=[vmem] * 4,
        out_specs=(vmem,) * 3,
        compiler_params=grant(16),
        cost_estimate=cost(4 * hid * feat * half_rays, 8 * hid * ray_total),
        name="near_rays",
    )(near, third_near, gathered, scale)
    pulled, terms, far_rays, far_scaled, *packs = pl.pallas_call(
        functools.partial(far_kernel, share, rays_of),
        out_shape=(f32(hid, ray_total), f32(1, ray_total), bf16(half_rays, feat), bf16(hid, half_rays))
        + (f32(pack_rows, feat),) * (tile_count - 1),
        in_specs=[vmem] * 8,
        out_specs=(vmem,) * (3 + tile_count),
        compiler_params=grant(16),
        cost_estimate=cost(0, 50 * feat * half_rays),
        name="far_rays",
    )(behind, far, third_near, gathered, scale, stats, near_pulled, near_terms)

    other_packs = from_others(packs)
    opened, third_near_grad, *mean = pl.pallas_call(
        functools.partial(weight_kernel, entries, height),
        out_shape=(f32(SAMPLES, ray_total), pltpu.VMEM((hid, feat), jnp.float32))
        + (f32(1, 128),) * int(packed),
        in_specs=[vmem] * 11,
        out_specs=(vmem,) * (2 + int(packed)),
        compiler_params=grant(16),
        cost_estimate=cost(0, 3 * hid * wide),
        name="weight_gradient",
    )(two, scale, kept, weights, pulled, terms, near, far, far_rays, far_scaled, partial)
    third_near_grad = pltpu.with_memory_space_constraint(third_near_grad, pltpu.VMEM)
    results = [(enc, hid), (hid, hid), (hid, feat), (1, hid), (decoder.shape[1], 1, feat)]
    first_grad, second_grad, third_grad, density_grad, decoder_grad = pl.pallas_call(
        functools.partial(backward_kernel, share),
        out_shape=tuple(f32(*shape) for shape in results),
        in_specs=[vmem] * (10 + tile_count),
        out_specs=(anywhere,) * len(results),
        scratch_shapes=[pltpu.VMEM((hid, ray_total), jnp.bfloat16)] * 2
        + [pltpu.VMEM(shape, jnp.float32) for shape in results[:2] + results[3:]]
        + [pltpu.SemaphoreType.DMA((len(results),))],
        compiler_params=grant(20),
        cost_estimate=cost(6 * hid * hid * wide, 10 * hid * wide),
        name="backward_tile",
    )(
        routed,
        one,
        two,
        steep,
        opened,
        weights,
        pulled,
        second,
        head,
        stats,
        third_near_grad,
        *other_packs,
    )

    mean_error = mean[0] if packed else lax.psum(error[0], ("depth", "lat", "core")) / entries
    return (
        first_grad[None, None],
        second_grad[None, None],
        third_grad[None, None],
        density_grad[None],
        jnp.transpose(decoder_grad, (1, 0, 2)),
        mean_error[0, 0],
    )


def solution(mesh):
    shape = mesh.devices.shape
    split = Mesh(
        mesh.devices.reshape(shape[0], shape[1] // PAIR, PAIR), ("depth", "lat", "core")
    )
    lateral = ("lat", "core")
    placed = (
        P("depth", lateral, None, None),
        P("depth", lateral, None, None),
        P("depth", lateral, None, None),
        P("depth", lateral, None, None),
        P("depth", lateral, None),
        P(lateral, None, None),
        P(lateral, None),
        P(lateral, None),
        P(lateral, None, "depth"),
    )
    return jax.shard_map(
        body,
        mesh=split,
        in_specs=placed,
        out_specs=(
            P("depth", lateral, None, None),
            P("depth", lateral, None, None),
            P("depth", lateral, None, None),
            P("depth", lateral, None),
            P(lateral, None, None),
            P(),
        ),
        check_vma=False,
    )
```
